768 devices in a mesh: group: 96 (over z, x, core), member: 8 (over y).
Axes of the slice: x: 4, y: 8, z: 12, core: 2. Of those that a mesh axis runs over, the one named last changes fastest.
Arguments:
- edge_field: float32 [2, 3072, 1024], P(None, 'group', 'member'), may hold values from -6 to 6
- conductance: float32 [2, 3072, 1024], P(None, 'group', 'member'), may hold values from 0.5 to 4
- send_index: int32 [768, 96, 5], P(('group', 'member')), may hold values from 0 to 8191
- panel_source: int32 [3072, 128], P(('group', 'member')), may hold values from 0 to 479, as said below
- surface_field: float32 [3072, 128], P(('group', 'member')), may hold values from -6 to 6
- near_columns: int32 [3072, 4], P(('group', 'member')), may hold values from 0 to 31
- near_tiles: float32 [3072, 4, 128, 128], P(('group', 'member')), may hold values from -0.25 to 0.25
- far_columns: int32 [3072, 16], P(('group', 'member')), may hold values from 0 to 3071
- far_ranks: int32 [3072, 16], P(('group', 'member')), may hold values from 8 to 32
- far_coupling: float32 [3072, 16, 32, 32], P(('group', 'member')), may hold values from -1 to 1
- basis_left: float32 [3072, 128, 32], P(('group', 'member')), may hold values from -1 to 1
- basis_right: float32 [3072, 128, 32], P(('group', 'member')), may hold values from -0.5 to 0.5
Outputs:
- volume_out: float32 [2, 3072, 1024], P(None, 'group', 'member')
- surface_out: float32 [3072, 128], P(('group', 'member'))
The draws below stay inside these ranges and needn't reach their ends.
Inputs may be any that keep to these rules, and one draw needn't show every extreme that they name: `panel_source`: on each device every one of the 480 trace slots is read by at least one of its panels.
All inputs are finite; a program needn't handle non-finite values.
Results may differ from the reference program's by a relative error of at most 0.000065.
Values sent between devices are 32-bit elements; how exact they have to be, the bound alone decides.
No kernel may reach another device: no remote copies, remote signals or barrier semaphores. Data moves between devices by JAX's collectives and lax.ppermute only.
A program may use at most 32 MiB of HBM per device.

```python
import math
import jax
import jax.numpy as jnp
from jax import lax

CX = 32
CY = 128
BS = 128
RANK = 32
NBLK = 4
NEAR = 4
FAR = 16
SLOT = 5
NX = 3072
NY = 1024
NBLOCKS = 3072
N_GROUP = 96
N_MEMBER = 8


def draw_panel_source(key, part):
    key = jax.random.fold_in(key, 7)
    device_count = NBLOCKS // NBLK
    panels = NBLK * BS
    total_slots = N_GROUP * SLOT
    key_upper, key_lower, key_perm = jax.random.split(key, 3)
    upper = jax.random.randint(key_upper, (device_count, panels), 0, total_slots)
    extra = jax.random.randint(key_lower, (device_count, panels), 0, upper + 1)
    position = jnp.arange(panels, dtype=jnp.int32)[None, :]
    base = jnp.where(position < total_slots, position, extra).astype(jnp.int32)
    perm_keys = jax.random.split(key_perm, device_count)
    shuffled = jax.vmap(lambda k, row: jax.random.permutation(k, row))(perm_keys, base)
    return shuffled.reshape(NBLOCKS, BS).astype(jnp.int32)


def with_ends(result, rng, low, high):
    longest = result.shape.index(max(result.shape))
    spots = []
    for shift in (0, 1):
        where = [jax.random.randint(jax.random.fold_in(rng, axis), (), 0, length) for axis, length in enumerate(result.shape)]
        where[longest] = (where[longest] + shift) % result.shape[longest]
        spots.append(tuple(where))
    return result.at[spots[0]].set(low).at[spots[1]].set(high)


def shard_levels(stream_key, extent, cuts, low, largest):
    loudness = 1.0
    for axis_at, blocks in cuts:
        heights = jax.random.uniform(jax.random.fold_in(jax.random.fold_in(stream_key, 6), axis_at), (blocks,), jnp.float32, low / len(cuts), largest / len(cuts))
        loudness = loudness * jnp.repeat(jnp.exp(heights), extent[axis_at] // blocks).reshape((-1,) + (1,) * (len(extent) - 1 - axis_at))
    return loudness


def centred(stream_key, extent, scale, reach, cuts=(), held_as=jnp.bfloat16):
    drawn = scale * jax.random.normal(stream_key, extent, jnp.float32)
    if cuts:
        drawn = drawn * shard_levels(stream_key, extent, cuts, -0.22, 0.18)
    return jnp.clip(drawn, -reach, reach).astype(held_as)


def setup_inputs(seed: int = 0) -> dict:
    splits = jax.random.split(jax.random.key(seed), 13)
    return {
        "edge_field": centred(splits[0], (2, NX, NY), 1.0, 6.0, ((1, 96), (2, 8)), jnp.float32),
        "conductance": jnp.clip(jnp.exp(math.log(4.0) - 2.0794415 * jax.random.uniform(splits[1], (2, NX, NY), jnp.float32) ** shard_levels(splits[1], (2, NX, NY), ((1, 96), (2, 8)), -0.2, 0.2)), 0.5, 4.0),
        "send_index": with_ends(jax.random.randint(splits[2], (NBLOCKS // NBLK, N_GROUP, SLOT), 0, 2 * CX * CY), jax.random.fold_in(splits[2], 1), 0, (2 * CX * CY) - 1).astype(jnp.int32),
        "panel_source": draw_panel_source(jax.random.fold_in(splits[12], 71), 0),
        "surface_field": centred(splits[4], (NBLOCKS, BS), 1.0, 6.0, ((0, 768),), jnp.float32),
        "near_columns": with_ends(jax.random.randint(splits[5], (NBLOCKS, NEAR), 0, N_MEMBER * NBLK), jax.random.fold_in(splits[5], 1), 0, (N_MEMBER * NBLK) - 1).astype(jnp.int32),
        "near_tiles": centred(splits[6], (NBLOCKS, NEAR, BS, BS), (NEAR * BS) ** -0.5, 0.25, ((0, 768),), jnp.float32),
        "far_columns": with_ends(jax.random.randint(splits[7], (NBLOCKS, FAR), 0, NBLOCKS), jax.random.fold_in(splits[7], 1), 0, NBLOCKS - 1).astype(jnp.int32),
        "far_ranks": with_ends(jax.random.randint(splits[8], (NBLOCKS, FAR), RANK // 4, RANK + 1), jax.random.fold_in(splits[8], 1), RANK // 4, RANK).astype(jnp.int32),
        "far_coupling": centred(splits[9], (NBLOCKS, FAR, RANK, RANK), RANK ** -0.5, 1.0, ((0, 768),), jnp.float32),
        "basis_left": centred(splits[10], (NBLOCKS, BS, RANK), RANK ** -0.5, 1.0, ((0, 768),), jnp.float32),
        "basis_right": centred(splits[11], (NBLOCKS, BS, RANK), BS ** -0.5, 0.5, ((0, 768),), jnp.float32),
    }


def apply_curl(edges, conduct):
    padded = jnp.pad(edges, ((0, 0), (1, 1), (1, 1)))
    edge_x = padded[0]
    edge_y = padded[1]
    flux = edge_y[1:, :-1] - edge_y[:-1, :-1] - edge_x[:-1, 1:] + edge_x[:-1, :-1]
    part_x = flux[1:, :-1] - flux[1:, 1:]
    part_y = flux[:-1, 1:] - flux[1:, 1:]
    return jnp.stack([part_x, part_y]) + conduct * edges


def reference(edge_field, conductance, send_index, panel_source, surface_field, near_columns, near_tiles, far_columns, far_ranks, far_coupling, basis_left, basis_right):
    groups = N_GROUP
    members = N_MEMBER
    local = 2 * CX * CY
    blocks = edge_field.reshape(2, groups, CX, members, CY).transpose(1, 3, 0, 2, 4).reshape(groups, members, local)
    sent = jnp.take_along_axis(blocks, send_index.reshape(groups, members, groups * SLOT), axis=2)
    received = sent.reshape(groups, members, groups, SLOT).transpose(2, 1, 0, 3).reshape(groups, members, groups * SLOT)
    source = panel_source.reshape(groups, members, NBLK * BS)
    trace = jnp.take_along_axis(received, source, axis=2).reshape(NBLOCKS, BS)
    highest = lax.Precision.HIGHEST
    per_group = members * NBLK
    offsets = (jnp.arange(NBLOCKS, dtype=jnp.int32) // per_group) * per_group
    vectors = surface_field[offsets[:, None] + near_columns]
    near_part = jnp.einsum('bnij,bnj->bi', near_tiles, vectors, precision=highest)
    coeffs = jnp.einsum('bkr,bk->br', basis_right, surface_field, precision=highest)
    gathered = coeffs[far_columns]
    keep = jnp.arange(RANK, dtype=jnp.int32)[None, None, :] < far_ranks[:, :, None]
    gathered = jnp.where(keep, gathered, jnp.float32(0.0))
    summed = jnp.einsum('bfrs,bfs->br', far_coupling, gathered, precision=highest)
    far_part = jnp.einsum('bkr,br->bk', basis_left, summed, precision=highest)
    surface_out = near_part + far_part + 0.5 * trace
    devices = groups * members
    shift_src = (jnp.arange(devices, dtype=jnp.int32) * (groups * SLOT)).reshape(groups, members, 1)
    returned = jax.ops.segment_sum(surface_field.reshape(-1), (source + shift_src).reshape(-1), num_segments=devices * groups * SLOT)
    arrived = returned.reshape(groups, members, groups, SLOT).transpose(2, 1, 0, 3).reshape(-1)
    shift_edge = (jnp.arange(devices, dtype=jnp.int32) * local).reshape(groups, members, 1)
    targets = (send_index.reshape(groups, members, groups * SLOT) + shift_edge).reshape(-1)
    added = jax.ops.segment_sum(arrived, targets, num_segments=devices * local)
    added = added.reshape(groups, members, 2, CX, CY).transpose(2, 0, 3, 1, 4).reshape(2, NX, NY)
    volume_out = apply_curl(edge_field, conductance) + added
    return volume_out, surface_out
```

```python
import functools

import jax
import jax.numpy as jnp
from jax import lax
from jax.experimental import pallas as pl
from jax.experimental.pallas import tpu as pltpu
from jax.sharding import PartitionSpec as P

F32 = jnp.float32
BF16 = jnp.bfloat16
ROWS = 4
EXTRA = 8


def split3(value):
    first = value.astype(BF16)
    rest = value - first.astype(F32)
    second = rest.astype(BF16)
    third = (rest - second.astype(F32)).astype(BF16)
    return first, second, third


def dot_exact(choice, value, dims):
    total = None
    for part in split3(value):
        term = lax.dot_general(choice, part, (dims, ((), ())), preferred_element_type=F32)
        total = term if total is None else total + term
    return total


def lanes(shape):
    return lax.broadcasted_iota(jnp.int32, shape, len(shape) - 1)


def rows(shape):
    return lax.broadcasted_iota(jnp.int32, shape, len(shape) - 2)


def pack_kernel(groups, slots, where_ref, edge_ref, send_ref, source_ref, surface_ref, right_ref, out_ref):
    blocks, width = surface_ref.shape
    rank = right_ref.shape[2]
    height = edge_ref.shape[1]
    group = where_ref[0]
    coeff = jnp.zeros((1, width), F32)
    for b in range(blocks):
        vector = surface_ref[b : b + 1, :]
        part = lax.dot_general(
            jnp.broadcast_to(vector, (8, width)),
            right_ref[b],
            (((1,), (0,)), ((), ())),
            precision=lax.Precision.HIGHEST,
            preferred_element_type=F32,
        )
        wide = jnp.concatenate([part] * (width // rank), axis=1)[0:1, :]
        coeff = jnp.where(lanes((1, width)) // rank == b, wide, coeff)
    out_ref[pl.ds(0, groups, stride=ROWS), :] = jnp.broadcast_to(coeff, (groups, width))
    edge_x = edge_ref[0]
    edge_y = edge_ref[1]
    last_x = edge_x[height - 1 : height, :]
    beyond = jnp.where(lanes((1, width)) == width - 1, 0.0, pltpu.roll(last_x, width - 1, 1))
    down = last_x - beyond - edge_y[height - 1 : height, :]
    up = edge_y[0:1, :]
    index = rows((groups, width))
    out_ref[pl.ds(1, groups, stride=ROWS), :] = jnp.where(index == group + 1, down, up)
    send = send_ref[0]
    flat = edge_ref[...].reshape(2 * height, width)
    lane = lanes((groups, width))
    tail = jnp.where(lane == 2 * slots, last_x[0:1, 0:1], 0.0)
    parts = split3(flat)
    for s in range(slots):
        column = send[:, s : s + 1]
        choice = (lanes((groups, 2 * height)) == column // width).astype(BF16)
        picked = None
        for part in parts:
            term = lax.dot_general(choice, part, (((1,), (0,)), ((), ())), preferred_element_type=F32)
            picked = term if picked is None else picked + term
        value = jnp.sum(jnp.where(lane == column % width, picked, 0.0), axis=1, keepdims=True)
        tail = jnp.where(lane == s, value, tail)
        total = jnp.zeros((groups, width), F32)
        slot = rows((groups, width)) * slots + s
        for b in range(blocks):
            total = total + jnp.where(source_ref[b : b + 1, :] == slot, surface_ref[b : b + 1, :], 0.0)
        tail = jnp.where(lane == slots + s, jnp.sum(total, axis=1, keepdims=True), tail)
    out_ref[pl.ds(2, groups, stride=ROWS), :] = tail
    out_ref[pl.ds(3, groups, stride=ROWS), :] = jnp.zeros((groups, width), F32)


def spread_kernel(groups, members, slots, where_ref, edge_ref, surface_ref, first_ref, out_ref):
    blocks, width = surface_ref.shape
    height = edge_ref.shape[1]
    group = where_ref[0]
    coeffs = first_ref[pl.ds(0, groups, stride=ROWS), :]
    below = first_ref[pl.ds(lax.min(group + 1, groups - 1) * ROWS + 1, 1), :]
    below = jnp.where(group + 1 < groups, below, 0.0)
    above = first_ref[pl.ds(lax.max(group - 1, 0) * ROWS + 2, 1), :]
    corner = jnp.where(group > 0, above[0:1, 2 * slots : 2 * slots + 1], 0.0)
    edge_x = edge_ref[0]
    edge_y = edge_ref[1]
    next_y = jnp.where(rows((height, width)) == height - 1, below, pltpu.roll(edge_y, height - 1, 0))
    flow = next_y - edge_y + edge_x
    last = (lanes((8, width)) == width - 1).astype(BF16)
    first = (lanes((8, width)) == 0).astype(BF16)
    ends = jnp.concatenate(
        [
            dot_exact(last, flow, ((1,), (1,)))[0:1, :],
            dot_exact(first, edge_x, ((1,), (1,)))[0:1, :],
            jnp.broadcast_to(corner, (1, width - 2 * height)),
        ],
        axis=1,
    )
    rim = jnp.concatenate([surface_ref[...], jnp.broadcast_to(ends, (EXTRA - blocks, width))], axis=0)
    for m in range(members):
        out_ref[m, 0:groups, :] = coeffs
        out_ref[m, groups : groups + EXTRA, :] = rim


def finish_kernel(
    groups,
    members,
    slots,
    where_ref,
    near_columns_ref,
    far_columns_ref,
    far_ranks_ref,
    edge_ref,
    conductance_ref,
    send_ref,
    source_ref,
    first_ref,
    second_ref,
    near_ref,
    coupling_ref,
    left_ref,
    volume_ref,
    surface_ref,
):
    blocks, width = source_ref.shape
    height = edge_ref.shape[1]
    rank = left_ref.shape[2]
    per_member = groups + EXTRA
    group = where_ref[0]
    member = where_ref[1]
    highest = lax.Precision.HIGHEST

    tail = first_ref[pl.ds(2, groups, stride=ROWS), :]
    ones_near = jnp.ones((8, width), F32)
    ones_far = jnp.ones((8, rank), F32)
    for b in range(blocks):
        total = jnp.zeros((width, width), F32)
        for n in range(near_ref.shape[1]):
            column = near_columns_ref[b, n]
            row = (column // blocks) * per_member + groups + column % blocks
            total = total + near_ref[b, n] * second_ref[pl.ds(row, 1), :]
        near = lax.dot_general(
            ones_near, total, (((1,), (1,)), ((), ())), precision=highest, preferred_element_type=F32
        )
        total = jnp.zeros((rank, rank), F32)
        for f in range(coupling_ref.shape[1]):
            column = far_columns_ref[b, f]
            device = column // blocks
            row = (device % members) * per_member + device // members
            picked = second_ref[pl.ds(row, 1), :]
            shift = (width - (column % blocks) * rank) % width
            picked = pltpu.roll(jnp.broadcast_to(picked, (8, width)), shift, 1)[0:1, :]
            picked = jnp.where(lanes((1, width)) < far_ranks_ref[b, f], picked, 0.0)
            total = total + coupling_ref[b, f] * picked[:, 0:rank]
        summed = lax.dot_general(
            ones_far, total, (((1,), (1,)), ((), ())), precision=highest, preferred_element_type=F32
        )
        far = lax.dot_general(
            summed, left_ref[b], (((1,), (1,)), ((), ())), precision=highest, preferred_element_type=F32
        )
        trace = jnp.zeros((groups, width), F32)
        for s in range(slots):
            slot = rows((groups, width)) * slots + s
            trace = trace + jnp.where(source_ref[b : b + 1, :] == slot, tail[:, s : s + 1], 0.0)
        trace = jnp.sum(trace, axis=0, keepdims=True)
        surface_ref[b : b + 1, :] = near[0:1, :] + far[0:1, :] + 0.5 * trace

    send = send_ref[0]
    added = None
    for s in range(slots):
        column = send[:, s : s + 1]
        choice = (lanes((groups, 2 * height)) == column // width).astype(BF16)
        value = jnp.where(lanes((groups, width)) == column % width, tail[:, slots + s : slots + s + 1], 0.0)
        term = dot_exact(choice, value, ((0,), (0,)))
        added = term if added is None else added + term

    edge_x = edge_ref[0]
    edge_y = edge_ref[1]
    shape = (height, width)
    lane = lanes(shape)
    line = rows(shape)
    below = first_ref[pl.ds(lax.min(group + 1, groups - 1) * ROWS + 1, 1), :]
    below = jnp.where(group + 1 < groups, below, 0.0)
    above = first_ref[pl.ds(lax.max(group - 1, 0) * ROWS + 1, 1), :]
    above = jnp.where(group > 0, above, 0.0)
    before = second_ref[pl.ds(lax.max(member - 1, 0) * per_member + groups + blocks, 1), :]
    before = jnp.where(member > 0, before, 0.0)
    after = second_ref[pl.ds(lax.min(member + 1, members - 1) * per_member + groups + blocks, 1), :]
    after = jnp.where(member + 1 < members, after, 0.0)

    def upright(row, start):
        wide = jnp.where(lanes((height, width)) == rows((height, width)) + start, row, 0.0)
        return jnp.sum(wide, axis=1, keepdims=True)

    next_x = jnp.where(lane == width - 1, upright(after, height), pltpu.roll(edge_x, width - 1, 1))
    next_y = jnp.where(line == height - 1, below, pltpu.roll(edge_y, height - 1, 0))
    flux = next_y - edge_y - next_x + edge_x
    left = upright(before, 0) - edge_x[:, 0:1]
    flux_left = jnp.where(lane == 0, left, pltpu.roll(flux, 1, 1))
    corner = after[0:1, 2 * height : 2 * height + 1]
    top = edge_y[0:1, :] + above - jnp.where(lanes((1, width)) == width - 1, corner, 0.0)
    flux_up = jnp.where(line == 0, top, pltpu.roll(flux, 1, 0))
    volume_ref[0] = flux_left - flux + conductance_ref[0] * edge_x + added[0:height, :]
    volume_ref[1] = flux_up - flux + conductance_ref[1] * edge_y + added[height : 2 * height, :]


def vmem(count):
    return [pl.BlockSpec(memory_space=pltpu.VMEM)] * count


def smem(count):
    return [pl.BlockSpec(memory_space=pltpu.SMEM)] * count


PARAMS = pltpu.CompilerParams(vmem_limit_bytes=16 * 1024 * 1024)


def body(
    edge_field,
    conductance,
    send_index,
    panel_source,
    surface_field,
    near_columns,
    near_tiles,
    far_columns,
    far_ranks,
    far_coupling,
    basis_left,
    basis_right,
):
    groups = lax.axis_size("group")
    members = lax.axis_size("member")
    slots = send_index.shape[2]
    blocks, width = surface_field.shape
    where = jnp.stack([lax.axis_index("group"), lax.axis_index("member")]).astype(jnp.int32)
    with jax.named_scope("pack"):
        first = pl.pallas_call(
            functools.partial(pack_kernel, groups, slots),
            out_shape=jax.ShapeDtypeStruct((groups * ROWS, width), F32),
            in_specs=smem(1) + vmem(5),
            out_specs=pl.BlockSpec(memory_space=pltpu.VMEM),
            compiler_params=PARAMS,
        )(where, edge_field, send_index, panel_source, surface_field, basis_right)
    first = lax.all_to_all(
        first.reshape(groups, ROWS, width), "group", split_axis=0, concat_axis=0, tiled=True
    ).reshape(groups * ROWS, width)
    with jax.named_scope("spread"):
        second = pl.pallas_call(
            functools.partial(spread_kernel, groups, members, slots),
            out_shape=jax.ShapeDtypeStruct((members, groups + EXTRA, width), F32),
            in_specs=smem(1) + vmem(3),
            out_specs=pl.BlockSpec(memory_space=pltpu.VMEM),
            compiler_params=PARAMS,
        )(where, edge_field, surface_field, first)
    second = lax.all_to_all(second, "member", split_axis=0, concat_axis=0, tiled=True)
    second = second.reshape(members * (groups + EXTRA), width)
    with jax.named_scope("finish"):
        return pl.pallas_call(
            functools.partial(finish_kernel, groups, members, slots),
            out_shape=(
                jax.ShapeDtypeStruct(edge_field.shape, F32),
                jax.ShapeDtypeStruct(surface_field.shape, F32),
            ),
            in_specs=smem(4) + vmem(9),
            out_specs=tuple(vmem(2)),
            compiler_params=PARAMS,
        )(
            where,
            near_columns,
            far_columns,
            far_ranks,
            edge_field,
            conductance,
            send_index,
            panel_source,
            first,
            second,
            near_tiles,
            far_coupling,
            basis_left,
        )


def solution(mesh):
    both = ("group", "member")
    placed = (
        P(None, "group", "member"),
        P(None, "group", "member"),
        P(both, None, None),
        P(both, None),
        P(both, None),
        P(both, None),
        P(both, None, None, None),
        P(both, None),
        P(both, None),
        P(both, None, None, None),
        P(both, None, None),
        P(both, None, None),
    )
    return jax.shard_map(
        body,
        mesh=mesh,
        in_specs=placed,
        out_specs=(P(None, "group", "member"), P(both, None)),
        check_vma=False,
    )
```

```python
import functools

import jax
import jax.numpy as jnp
from jax import lax
from jax.experimental import pallas as pl
from jax.experimental.pallas import tpu as pltpu
from jax.sharding import PartitionSpec as P

F32 = jnp.float32
BF16 = jnp.bfloat16
ROWS = 4
EXTRA = 8


def split3(value):
    first = value.astype(BF16)
    rest = value - first.astype(F32)
    second = rest.astype(BF16)
    third = (rest - second.astype(F32)).astype(BF16)
    return first, second, third


def dot_exact(choice, value, dims):
    total = None
    for part in split3(value):
        term = lax.dot_general(choice, part, (dims, ((), ())), preferred_element_type=F32)
        total = term if total is None else total + term
    return total


def lanes(shape):
    return lax.broadcasted_iota(jnp.int32, shape, len(shape) - 1)


def rows(shape):
    return lax.broadcasted_iota(jnp.int32, shape, len(shape) - 2)


def pack_kernel(groups, slots, where_ref, edge_ref, send_ref, source_ref, surface_ref, right_ref, out_ref):
    blocks, width = surface_ref.shape
    rank = right_ref.shape[1]
    height = edge_ref.shape[1]
    group = where_ref[0]
    every = lax.dot_general(
        surface_ref[...],
        right_ref[...].reshape(blocks * rank, width),
        (((1,), (1,)), ((), ())),
        precision=lax.Precision.HIGHEST,
        preferred_element_type=F32,
    )
    own = lanes((blocks, blocks * rank)) // rank == rows((blocks, blocks * rank))
    coeff = jnp.sum(jnp.where(own, every, 0.0), axis=0, keepdims=True)
    out_ref[pl.ds(0, groups, stride=ROWS), :] = jnp.broadcast_to(coeff, (groups, width))
    edge_x = edge_ref[0]
    edge_y = edge_ref[1]
    last_x = edge_x[height - 1 : height, :]
    beyond = jnp.where(lanes((1, width)) == width - 1, 0.0, pltpu.roll(last_x, width - 1, 1))
    down = last_x - beyond - edge_y[height - 1 : height, :]
    up = edge_y[0:1, :]
    index = rows((groups, width))
    out_ref[pl.ds(1, groups, stride=ROWS), :] = jnp.where(index == group + 1, down, up)
    send = send_ref[0]
    flat = edge_ref[...].reshape(2 * height, width)
    lane = lanes((groups, width))
    tail = jnp.where(lane == 2 * slots, last_x[0:1, 0:1], 0.0)
    parts = split3(flat)
    for s in range(slots):
        column = send[:, s : s + 1]
        choice = (lanes((groups, 2 * height)) == column // width).astype(BF16)
        picked = None
        for part in parts:
            term = lax.dot_general(choice, part, (((1,), (0,)), ((), ())), preferred_element_type=F32)
            picked = term if picked is None else picked + term
        value = jnp.sum(jnp.where(lane == column % width, picked, 0.0), axis=1, keepdims=True)
        tail = jnp.where(lane == s, value, tail)
        total = jnp.zeros((groups, width), F32)
        slot = rows((groups, width)) * slots + s
        for b in range(blocks):
            total = total + jnp.where(source_ref[b : b + 1, :] == slot, surface_ref[b : b + 1, :], 0.0)
        tail = jnp.where(lane == slots + s, jnp.sum(total, axis=1, keepdims=True), tail)
    out_ref[pl.ds(2, groups, stride=ROWS), :] = tail
    out_ref[pl.ds(3, groups, stride=ROWS), :] = jnp.zeros((groups, width), F32)


def spread_kernel(groups, members, slots, where_ref, edge_ref, surface_ref, first_ref, out_ref):
    blocks, width = surface_ref.shape
    height = edge_ref.shape[1]
    group = where_ref[0]
    coeffs = first_ref[pl.ds(0, groups, stride=ROWS), :]
    below = first_ref[pl.ds(lax.min(group + 1, groups - 1) * ROWS + 1, 1), :]
    below = jnp.where(group + 1 < groups, below, 0.0)
    above = first_ref[pl.ds(lax.max(group - 1, 0) * ROWS + 2, 1), :]
    corner = jnp.where(group > 0, above[0:1, 2 * slots : 2 * slots + 1], 0.0)
    edge_x = edge_ref[0]
    edge_y = edge_ref[1]
    next_y = jnp.where(rows((height, width)) == height - 1, below, pltpu.roll(edge_y, height - 1, 0))
    flow = next_y - edge_y + edge_x
    last = (lanes((8, width)) == width - 1).astype(BF16)
    first = (lanes((8, width)) == 0).astype(BF16)
    ends = jnp.concatenate(
        [
            dot_exact(last, flow, ((1,), (1,)))[0:1, :],
            dot_exact(first, edge_x, ((1,), (1,)))[0:1, :],
            jnp.broadcast_to(corner, (1, width - 2 * height)),
        ],
        axis=1,
    )
    rim = jnp.concatenate([surface_ref[...], jnp.broadcast_to(ends, (EXTRA - blocks, width))], axis=0)
    for m in range(members):
        out_ref[m, 0:groups, :] = coeffs
        out_ref[m, groups : groups + EXTRA, :] = rim


def finish_kernel(
    groups,
    members,
    slots,
    where_ref,
    near_columns_ref,
    far_columns_ref,
    far_ranks_ref,
    edge_ref,
    conductance_ref,
    send_ref,
    source_ref,
    first_ref,
    second_ref,
    near_ref,
    coupling_ref,
    left_ref,
    volume_ref,
    surface_ref,
):
    blocks, width = source_ref.shape
    height = edge_ref.shape[1]
    rank = left_ref.shape[1]
    per_member = groups + EXTRA
    group = where_ref[0]
    member = where_ref[1]
    highest = lax.Precision.HIGHEST

    tail = first_ref[pl.ds(2, groups, stride=ROWS), :]
    sums = []
    fars = []
    for b in range(blocks):
        total = jnp.zeros((width, width), F32)
        for n in range(near_ref.shape[1]):
            column = near_columns_ref[b, n]
            row = (column // blocks) * per_member + groups + column % blocks
            total = total + near_ref[b, n] * second_ref[pl.ds(row, 1), :]
        sums.append(total)
        total = jnp.zeros((rank, rank), F32)
        for f in range(coupling_ref.shape[1]):
            column = far_columns_ref[b, f]
            device = column // blocks
            row = (device % members) * per_member + device // members
            picked = second_ref[pl.ds(row, 1), :]
            shift = (width - (column % blocks) * rank) % width
            picked = pltpu.roll(jnp.broadcast_to(picked, (8, width)), shift, 1)[0:1, :]
            picked = jnp.where(lanes((1, width)) < far_ranks_ref[b, f], picked, 0.0)
            total = total + coupling_ref[b, f] * picked[:, 0:rank]
        fars.append(total)
    near = lax.dot_general(
        jnp.ones((8, width), F32),
        jnp.concatenate(sums, axis=0),
        (((1,), (1,)), ((), ())),
        precision=highest,
        preferred_element_type=F32,
    )
    summed = lax.dot_general(
        jnp.ones((8, rank), F32),
        jnp.concatenate(fars, axis=0),
        (((1,), (1,)), ((), ())),
        precision=highest,
        preferred_element_type=F32,
    )
    own = lanes(summed.shape) // rank == rows(summed.shape)
    far = lax.dot_general(
        jnp.where(own, summed, 0.0),
        left_ref[...].reshape(blocks * rank, width),
        (((1,), (0,)), ((), ())),
        precision=highest,
        preferred_element_type=F32,
    )
    for b in range(blocks):
        trace = jnp.zeros((groups, width), F32)
        for s in range(slots):
            slot = rows((groups, width)) * slots + s
            trace = trace + jnp.where(source_ref[b : b + 1, :] == slot, tail[:, s : s + 1], 0.0)
        trace = jnp.sum(trace, axis=0, keepdims=True)
        surface_ref[b : b + 1, :] = near[0:1, b * width : (b + 1) * width] + far[b : b + 1, :] + 0.5 * trace

    send = send_ref[0]
    added = None
    for s in range(slots):
        column = send[:, s : s + 1]
        choice = (lanes((groups, 2 * height)) == column // width).astype(BF16)
        value = jnp.where(lanes((groups, width)) == column % width, tail[:, slots + s : slots + s + 1], 0.0)
        term = dot_exact(choice, value, ((0,), (0,)))
        added = term if added is None else added + term

    edge_x = edge_ref[0]
    edge_y = edge_ref[1]
    shape = (height, width)
    lane = lanes(shape)
    line = rows(shape)
    below = first_ref[pl.ds(lax.min(group + 1, groups - 1) * ROWS + 1, 1), :]
    below = jnp.where(group + 1 < groups, below, 0.0)
    above = first_ref[pl.ds(lax.max(group - 1, 0) * ROWS + 1, 1), :]
    above = jnp.where(group > 0, above, 0.0)
    before = second_ref[pl.ds(lax.max(member - 1, 0) * per_member + groups + blocks, 1), :]
    before = jnp.where(member > 0, before, 0.0)
    after = second_ref[pl.ds(lax.min(member + 1, members - 1) * per_member + groups + blocks, 1), :]
    after = jnp.where(member + 1 < members, after, 0.0)

    def upright(row, start):
        wide = jnp.where(lanes((height, width)) == rows((height, width)) + start, row, 0.0)
        return jnp.sum(wide, axis=1, keepdims=True)

    next_x = jnp.where(lane == width - 1, upright(after, height), pltpu.roll(edge_x, width - 1, 1))
    next_y = jnp.where(line == height - 1, below, pltpu.roll(edge_y, height - 1, 0))
    flux = next_y - edge_y - next_x + edge_x
    left = upright(before, 0) - edge_x[:, 0:1]
    flux_left = jnp.where(lane == 0, left, pltpu.roll(flux, 1, 1))
    corner = after[0:1, 2 * height : 2 * height + 1]
    top = edge_y[0:1, :] + above - jnp.where(lanes((1, width)) == width - 1, corner, 0.0)
    flux_up = jnp.where(line == 0, top, pltpu.roll(flux, 1, 0))
    volume_ref[0] = flux_left - flux + conductance_ref[0] * edge_x + added[0:height, :]
    volume_ref[1] = flux_up - flux + conductance_ref[1] * edge_y + added[height : 2 * height, :]


def vmem(count):
    return [pl.BlockSpec(memory_space=pltpu.VMEM)] * count


def smem(count):
    return [pl.BlockSpec(memory_space=pltpu.SMEM)] * count


PARAMS = pltpu.CompilerParams(vmem_limit_bytes=16 * 1024 * 1024)


def body(
    edge_field,
    conductance,
    send_index,
    panel_source,
    surface_field,
    near_columns,
    near_tiles,
    far_columns,
    far_ranks,
    far_coupling,
    basis_left,
    basis_right,
):
    groups = lax.axis_size("group")
    members = lax.axis_size("member")
    slots = send_index.shape[2]
    blocks, width = surface_field.shape
    where = jnp.stack([lax.axis_index("group"), lax.axis_index("member")]).astype(jnp.int32)
    with jax.named_scope("pack"):
        first = pl.pallas_call(
            functools.partial(pack_kernel, groups, slots),
            out_shape=jax.ShapeDtypeStruct((groups * ROWS, width), F32),
            in_specs=smem(1) + vmem(5),
            out_specs=pl.BlockSpec(memory_space=pltpu.VMEM),
            compiler_params=PARAMS,
        )(where, edge_field, send_index, panel_source, surface_field, jnp.swapaxes(basis_right, 1, 2))
    first = lax.all_to_all(
        first.reshape(groups, ROWS, width), "group", split_axis=0, concat_axis=0, tiled=True
    ).reshape(groups * ROWS, width)
    with jax.named_scope("spread"):
        second = pl.pallas_call(
            functools.partial(spread_kernel, groups, members, slots),
            out_shape=jax.ShapeDtypeStruct((members, groups + EXTRA, width), F32),
            in_specs=smem(1) + vmem(3),
            out_specs=pl.BlockSpec(memory_space=pltpu.VMEM),
            compiler_params=PARAMS,
        )(where, edge_field, surface_field, first)
    second = lax.all_to_all(second, "member", split_axis=0, concat_axis=0, tiled=True)
    second = second.reshape(members * (groups + EXTRA), width)
    with jax.named_scope("finish"):
        return pl.pallas_call(
            functools.partial(finish_kernel, groups, members, slots),
            out_shape=(
                jax.ShapeDtypeStruct(edge_field.shape, F32),
                jax.ShapeDtypeStruct(surface_field.shape, F32),
            ),
            in_specs=smem(4) + vmem(9),
            out_specs=tuple(vmem(2)),
            compiler_params=PARAMS,
        )(
            where,
            near_columns,
            far_columns,
            far_ranks,
            edge_field,
            conductance,
            send_index,
            panel_source,
            first,
            second,
            near_tiles,
            far_coupling,
            jnp.swapaxes(basis_left, 1, 2),
        )


def solution(mesh):
    both = ("group", "member")
    placed = (
        P(None, "group", "member"),
        P(None, "group", "member"),
        P(both, None, None),
        P(both, None),
        P(both, None),
        P(both, None),
        P(both, None, None, None),
        P(both, None),
        P(both, None),
        P(both, None, None, None),
        P(both, None, None),
        P(both, None, None),
    )
    return jax.shard_map(
        body,
        mesh=mesh,
        in_specs=placed,
        out_specs=(P(None, "group", "member"), P(both, None)),
        check_vma=False,
    )
```

```python
import functools

import jax
import jax.numpy as jnp
from jax import lax
from jax.experimental import pallas as pl
from jax.experimental.pallas import tpu as pltpu
from jax.sharding import PartitionSpec as P

F32 = jnp.float32
BF16 = jnp.bfloat16
HIGHEST = lax.Precision.HIGHEST
CORES = 2
ROWS = 3
EXTRA = 8
SIDE = 8


def split3(value):
    first = value.astype(BF16)
    rest = value - first.astype(F32)
    second = rest.astype(BF16)
    third = (rest - second.astype(F32)).astype(BF16)
    return first, second, third


def dot_exact(choice, value, dims):
    total = None
    for part in split3(value):
        term = lax.dot_general(choice, part, (dims, ((), ())), preferred_element_type=F32)
        total = term if total is None else total + term
    return total


def dot_full(left, right, dims):
    return lax.dot_general(left, right, (dims, ((), ())), precision=HIGHEST, preferred_element_type=F32)


def lanes(shape):
    return lax.broadcasted_iota(jnp.int32, shape, len(shape) - 1)


def rows(shape):
    return lax.broadcasted_iota(jnp.int32, shape, len(shape) - 2)


def upright(row, start, shape):
    wide = jnp.where(lanes(shape) == rows(shape) + start, row, 0.0)
    return jnp.sum(wide, axis=1, keepdims=True)


def fetch(pairs, sems):
    copies = [pltpu.make_async_copy(source, target, sems.at[i]) for i, (source, target) in enumerate(pairs)]
    for copy in copies:
        copy.start()
    return copies


def pack_kernel(
    edge_in,
    send_in,
    source_in,
    surface_in,
    right_in,
    out_ref,
    rim_ref,
    edge_ref,
    send_ref,
    source_ref,
    surface_ref,
    right_ref,
    tail_ref,
    sems,
):
    blocks, width = surface_ref.shape
    rank = right_ref.shape[1]
    height = edge_ref.shape[1]
    slots, _, groups = send_ref.shape
    chips = groups // CORES
    copies = fetch(
        (
            (surface_in, surface_ref),
            (right_in, right_ref),
            (edge_in, edge_ref),
            (send_in, send_ref),
            (source_in, source_ref),
        ),
        sems,
    )
    for copy in copies:
        copy.wait()
    core = lax.rem(lax.axis_index("group"), CORES)
    every = dot_full(surface_ref[...], right_ref[...].reshape(blocks * rank, width), ((1,), (1,)))
    own = lanes((blocks, blocks * rank)) // rank == rows((blocks, blocks * rank))
    coeff = jnp.sum(jnp.where(own, every, 0.0), axis=0, keepdims=True)
    out_ref[pl.ds(0, chips, stride=ROWS), :] = jnp.broadcast_to(coeff, (chips, width))
    edge_x = edge_ref[0]
    edge_y = edge_ref[1]
    last_x = edge_x[height - 1 : height, :]
    beyond = jnp.where(lanes((1, width)) == width - 1, 0.0, pltpu.roll(last_x, width - 1, 1))
    down = last_x - beyond - edge_y[height - 1 : height, :]
    rim = jnp.where(core == CORES - 1, down, edge_y[0:1, :])
    out_ref[pl.ds(1, chips, stride=ROWS), :] = jnp.broadcast_to(rim, (chips, width))
    next_y = jnp.where(rows((height, width)) == height - 1, 0.0, pltpu.roll(edge_y, height - 1, 0))
    flow = next_y - edge_y + edge_x
    last = (lanes((8, width)) == width - 1).astype(BF16)
    first = (lanes((8, width)) == 0).astype(BF16)
    ends = jnp.concatenate(
        [
            dot_exact(last, flow, ((1,), (1,)))[0:1, :],
            dot_exact(first, edge_x, ((1,), (1,)))[0:1, :],
            jnp.broadcast_to(edge_y[0:1, width - 1 : width], (1, width - 2 * height)),
        ],
        axis=1,
    )
    own = jnp.where(core == 0, down, edge_y[0:1, :])
    rim_ref[0:blocks, :] = surface_ref[...]
    rim_ref[blocks : blocks + 1, :] = ends
    rim_ref[blocks + 1 :, :] = jnp.broadcast_to(own, (EXTRA - blocks - 1, width))
    index = jnp.concatenate(
        [send_ref[s] for s in range(slots)] + [jnp.zeros((8 - slots, groups), jnp.int32)], axis=0
    ).T
    parts = split3(edge_ref[...].reshape(2 * height, width))
    lane = lanes((groups, width))
    tail = jnp.where(lane == 2 * CORES * slots, last_x[0:1, 0:1], 0.0)
    for s in range(slots):
        column = index[:, s : s + 1]
        choice = (lanes((groups, 2 * height)) == column // width).astype(BF16)
        picked = None
        for part in parts:
            term = lax.dot_general(choice, part, (((1,), (0,)), ((), ())), preferred_element_type=F32)
            picked = term if picked is None else picked + term
        value = jnp.sum(jnp.where(lane == column % width, picked, 0.0), axis=1, keepdims=True)
        tail = jnp.where(lane == s, value, tail)
        total = jnp.zeros((groups, width), F32)
        slot = rows((groups, width)) * slots + s
        for b in range(blocks):
            total = total + jnp.where(source_ref[b : b + 1, :] == slot, surface_ref[b : b + 1, :], 0.0)
        tail = jnp.where(lane == slots + s, jnp.sum(total, axis=1, keepdims=True), tail)
    tail_ref[...] = tail
    even = tail_ref[pl.ds(0, chips, stride=CORES), :]
    odd = tail_ref[pl.ds(1, chips, stride=CORES), :]
    lane = lanes((chips, width))
    moved = pltpu.roll(odd, 2 * slots, 1)
    mine = (lane >= 2 * slots) & (lane < 2 * CORES * slots)
    out_ref[pl.ds(2, chips, stride=ROWS), :] = jnp.where(mine, moved, even)


def spread_kernel(members, slots, first_ref, rim_ref, out_ref, side_ref):
    width = rim_ref.shape[1]
    chips = first_ref.shape[0] // ROWS
    blocks = EXTRA // 2
    group = lax.axis_index("group")
    core = lax.rem(group, CORES)
    chip = group // CORES
    before = jnp.where(chip > 0, 1.0, 0.0)
    after = jnp.where(chip + 1 < chips, 1.0, 0.0)
    chip_before = lax.max(chip - 1, 0) * ROWS
    chip_after = lax.min(chip + 1, chips - 1) * ROWS
    rim_before = first_ref[pl.ds(chip_before + 1, 1), :] * before
    rim_after = first_ref[pl.ds(chip_after + 1, 1), :] * after
    corner_before = first_ref[pl.ds(chip_before + 2, 1), :] * before
    corners = 2 * CORES * slots
    lane = lanes((EXTRA, width))
    line = rows((EXTRA, width))
    rim = rim_ref[...]
    corner = jnp.where(lane < 7 * width // 8, corner_before[0:1, corners : corners + 1], rim_after[0:1, width - 1 : width])
    rim = jnp.where((line == blocks) & (lane >= 3 * width // 4), corner, rim)
    coeffs = first_ref[pl.ds(0, chips, stride=ROWS), :]
    for m in range(members):
        out_ref[m, 0:chips, :] = coeffs
        out_ref[m, chips : chips + EXTRA, :] = rim
    other = jnp.where(core == 0, rim_after, rim_before)
    side_ref[0:chips, :] = first_ref[pl.ds(2, chips, stride=ROWS), :]
    half = rows((SIDE, width)) < SIDE // 2
    side_ref[chips : chips + SIDE, :] = jnp.where(half, rim[blocks + 1 : blocks + 2, :], other)


def local_kernel(
    members,
    edge_in,
    conductance_in,
    send_in,
    source_in,
    near_columns_in,
    far_columns_in,
    far_ranks_in,
    coupling_in,
    left_in,
    side_ref,
    volume_ref,
    trace_ref,
    index_ref,
    keep_ref,
    near_pick_ref,
    coupling_ref,
    left_ref,
    edge_ref,
    conductance_ref,
    send_ref,
    source_ref,
    near_columns_ref,
    far_columns_ref,
    far_ranks_ref,
    tail_ref,
    sems,
):
    copies = fetch(
        (
            (edge_in, edge_ref),
            (conductance_in, conductance_ref),
            (send_in, send_ref),
            (source_in, source_ref),
            (near_columns_in, near_columns_ref),
            (far_columns_in, far_columns_ref),
            (far_ranks_in, far_ranks_ref),
            (left_in, left_ref),
            (coupling_in, coupling_ref),
        ),
        sems,
    )
    for copy in copies[:-2]:
        copy.wait()
    blocks, width = source_ref.shape
    height = edge_ref.shape[1]
    slots, _, groups = send_ref.shape
    chips = groups // CORES
    rank = left_ref.shape[1]
    core = lax.rem(lax.axis_index("group"), CORES)
    near_count = near_columns_ref.shape[1]
    far_count = far_columns_ref.shape[1]
    column = far_columns_ref[...]
    device = column // blocks
    group = device // members
    per_member = chips + EXTRA
    place = (group % CORES) * (members * per_member) + (device % members) * per_member + group // CORES
    index_ref[...] = jnp.zeros(index_ref.shape, jnp.int32)
    index_ref[0:blocks, 0:far_count] = place
    lane = lanes((far_count, width))
    for b in range(blocks):
        square = (far_count, far_count)
        side = lanes(square) == rows(square)
        packed = column[b : b + 1, :] % blocks * width + far_ranks_ref[b : b + 1, :]
        packed = jnp.sum(jnp.where(side, packed, 0).astype(F32), axis=1, keepdims=True).astype(jnp.int32)
        kept = (lane // rank == packed // width) & (lane % rank < packed % width)
        keep_ref[b * far_count : (b + 1) * far_count, :] = kept.astype(F32)
        square = (near_count, near_count)
        side = lanes(square) == rows(square)
        picked = jnp.where(side, near_columns_ref[b : b + 1, :], 0).astype(F32)
        picked = jnp.sum(picked, axis=1, keepdims=True).astype(jnp.int32)
        near_pick_ref[b * near_count : (b + 1) * near_count, :] = (lanes((near_count, width)) == picked).astype(F32)
    for c in range(CORES):
        half = side_ref[c, 0:chips, :]
        half = jnp.where(core == 0, half, pltpu.roll(half, width - 2 * slots, 1))
        tail_ref[pl.ds(c, chips, stride=CORES), :] = half
    tail = tail_ref[...]
    for b in range(blocks):
        trace = jnp.zeros((groups, width), F32)
        for s in range(slots):
            slot = rows((groups, width)) * slots + s
            trace = trace + jnp.where(source_ref[b : b + 1, :] == slot, tail[:, s : s + 1], 0.0)
        trace_ref[b : b + 1, :] = 0.5 * jnp.sum(trace, axis=0, keepdims=True)
    index = jnp.concatenate(
        [send_ref[s] for s in range(slots)] + [jnp.zeros((8 - slots, groups), jnp.int32)], axis=0
    ).T
    added = None
    for s in range(slots):
        column = index[:, s : s + 1]
        choice = (lanes((groups, 2 * height)) == column // width).astype(BF16)
        value = jnp.where(lanes((groups, width)) == column % width, tail[:, slots + s : slots + s + 1], 0.0)
        term = dot_exact(choice, value, ((0,), (0,)))
        added = term if added is None else added + term
    edge_x = edge_ref[0]
    edge_y = edge_ref[1]
    shape = (height, width)
    lane = lanes(shape)
    line = rows(shape)
    own = side_ref[1 - core, chips : chips + 1, :]
    other = side_ref[1 - core, chips + SIDE // 2 : chips + SIDE // 2 + 1, :]
    above = jnp.where(core == 0, other, own)
    below = jnp.where(core == 0, own, other)
    next_x = jnp.where(lane == width - 1, 0.0, pltpu.roll(edge_x, width - 1, 1))
    next_y = jnp.where(line == height - 1, below, pltpu.roll(edge_y, height - 1, 0))
    flux = next_y - edge_y - next_x + edge_x
    flux_left = jnp.where(lane == 0, -edge_x, pltpu.roll(flux, 1, 1))
    flux_up = jnp.where(line == 0, edge_y + above, pltpu.roll(flux, 1, 0))
    volume_ref[0] = flux_left - flux + conductance_ref[0] * edge_x + added[0:height, :]
    volume_ref[1] = flux_up - flux + conductance_ref[1] * edge_y + added[height : 2 * height, :]
    for copy in copies[-2:]:
        copy.wait()


def finish_kernel(
    members,
    chips,
    volume_in,
    trace_ref,
    index_in,
    keep_ref,
    near_pick_ref,
    every_ref,
    near_ref,
    coupling_ref,
    left_ref,
    volume_ref,
    surface_ref,
    index_ref,
    picked_ref,
    vector_ref,
    sem,
):
    blocks, width = trace_ref.shape
    height = volume_ref.shape[1]
    rank = left_ref.shape[1]
    per_member = chips + EXTRA
    per_core = members * per_member
    core = lax.rem(lax.axis_index("group"), CORES)
    member = lax.axis_index("member")
    copy = pltpu.make_async_copy(index_in, index_ref, sem)
    copy.start()
    near_count = near_ref.shape[1]
    far_count = coupling_ref.shape[1]
    fields = [every_ref[pl.ds(core * per_core + m * per_member + chips, EXTRA), :][0:blocks, :] for m in range(members)]
    choice = near_pick_ref[:, 0 : members * blocks].astype(BF16)
    vector_ref[...] = dot_exact(choice, jnp.concatenate(fields, axis=0), ((1,), (0,)))
    sums = []
    for b in range(blocks):
        total = jnp.zeros((width, width), F32)
        for n in range(near_count):
            at = b * near_count + n
            total = total + near_ref[b, n] * vector_ref[at : at + 1, :]
        sums.append(total)
    near = dot_exact(jnp.ones((8, width), BF16), jnp.concatenate(sums, axis=0), ((1,), (1,)))
    copy.wait()
    for b in range(blocks):
        for f in range(far_count):
            picked_ref[b * far_count + f : b * far_count + f + 1, :] = every_ref[pl.ds(index_ref[b, f], 1), :]
    picked = jnp.where(keep_ref[...] > 0.0, picked_ref[...], 0.0)
    folded = picked
    for q in range(1, width // rank):
        folded = folded + pltpu.roll(picked, q * rank, 1)
    picked_ref[...] = folded
    for b in range(blocks):
        total = jnp.zeros((rank, rank), F32)
        for f in range(far_count):
            at = b * far_count + f
            total = total + coupling_ref[b, f] * picked_ref[at : at + 1, 0:rank]
        summed = jnp.sum(total, axis=1, keepdims=True)
        far = jnp.sum(left_ref[b] * summed, axis=0, keepdims=True)
        surface_ref[b : b + 1, :] = near[0:1, b * width : (b + 1) * width] + far + trace_ref[b : b + 1, :]

    ends = chips + blocks
    before = lax.max(member - 1, 0) * per_member + ends
    after = lax.min(member + 1, members - 1) * per_member + ends
    inside = jnp.where(member > 0, 1.0, 0.0)
    mine = every_ref[pl.ds(core * per_core + before, 1), :] * inside
    theirs = every_ref[pl.ds((1 - core) * per_core + before, 1), :] * inside
    inside = jnp.where(member + 1 < members, 1.0, 0.0)
    mine_after = every_ref[pl.ds(core * per_core + after, 1), :] * inside
    theirs_after = every_ref[pl.ds((1 - core) * per_core + after, 1), :] * inside
    shape = (height, width)
    lane = lanes(shape)
    line = rows(shape)
    corner_y = 2 * height + jnp.where(core == 0, 0, 3 * height // 2)
    left = upright(mine, 0, shape)
    left = left + jnp.where(line[:, 0:1] == height - 1, upright(theirs, corner_y - height + 1, shape), 0.0)
    right = upright(mine_after, height, shape)
    corner_x = jnp.where(core == 0, 3 * height, 2 * height - 1)
    corner = jnp.sum(jnp.where(lanes((1, width)) == corner_x, theirs_after, 0.0), axis=1, keepdims=True)
    end = jnp.where(lane == width - 1, right, 0.0)
    volume_ref[0] = volume_in[0] + jnp.where(lane == 0, left, 0.0) + end
    last = jnp.where(lane == width - 1, 1.0, 0.0)
    up = jnp.where(line == 0, corner, pltpu.roll(jnp.broadcast_to(right, shape), 1, 0))
    volume_ref[1] = volume_in[1] + end - last * up


def vmem(count):
    return [pl.BlockSpec(memory_space=pltpu.VMEM)] * count


PARAMS = pltpu.CompilerParams(vmem_limit_bytes=16 * 1024 * 1024)


def body(
    edge_field,
    conductance,
    send_index,
    panel_source,
    surface_field,
    near_columns,
    near_tiles,
    far_columns,
    far_ranks,
    far_coupling,
    basis_left,
    basis_right,
):
    groups = lax.axis_size("group")
    members = lax.axis_size("member")
    slots = send_index.shape[2]
    blocks, width = surface_field.shape
    chips = groups // CORES
    send = jnp.transpose(send_index, (2, 0, 1))
    right = jnp.swapaxes(basis_right, 1, 2)
    left = jnp.swapaxes(basis_left, 1, 2)
    near_count = near_columns.shape[1]
    far_count = far_columns.shape[1]
    one_core = [[chip * CORES + core for chip in range(chips)] for core in range(CORES)]
    one_chip = [[chip * CORES + core for core in range(CORES)] for chip in range(chips)]

    hbm = pl.BlockSpec(memory_space=pltpu.HBM)
    edge_field, conductance, send, panel_source, surface_field, right, left, far_coupling = [
        pltpu.with_memory_space_constraint(array, pltpu.HBM)
        for array in (edge_field, conductance, send, panel_source, surface_field, right, left, far_coupling)
    ]
    near_columns, far_columns, far_ranks = [
        pltpu.with_memory_space_constraint(array, pltpu.HBM) for array in (near_columns, far_columns, far_ranks)
    ]

    def like(array):
        return pltpu.VMEM(array.shape, array.dtype)

    def out(*shape, dtype=F32):
        return jax.ShapeDtypeStruct(shape, dtype)

    first, rim = pl.pallas_call(
        pack_kernel,
        name="pack",
        out_shape=(out(chips * ROWS, width), out(EXTRA, width)),
        in_specs=[hbm] * 5,
        out_specs=tuple(vmem(2)),
        scratch_shapes=[
            like(edge_field),
            like(send),
            like(panel_source),
            like(surface_field),
            like(right),
            pltpu.VMEM((groups, width), F32),
            pltpu.SemaphoreType.DMA((5,)),
        ],
        compiler_params=PARAMS,
    )(edge_field, send, panel_source, surface_field, right)
    first = lax.all_to_all(
        first.reshape(chips, 1, ROWS * width),
        "group",
        split_axis=0,
        concat_axis=0,
        axis_index_groups=one_core,
        tiled=True,
    ).reshape(chips * ROWS, width)
    second, side = pl.pallas_call(
        functools.partial(spread_kernel, members, slots),
        name="spread",
        out_shape=(out(members, chips + EXTRA, width), out(chips + SIDE, width)),
        in_specs=vmem(2),
        out_specs=tuple(vmem(2)),
        compiler_params=PARAMS,
    )(first, rim)
    second = lax.all_to_all(second, "member", split_axis=0, concat_axis=0, tiled=True)
    side = lax.all_gather(side, "group", axis=0, axis_index_groups=one_chip, tiled=True)
    volume, trace, index, keep, near_pick, coupling, left = pl.pallas_call(
        functools.partial(local_kernel, members),
        name="local",
        out_shape=(
            out(*edge_field.shape),
            out(blocks, width),
            out(8, width, dtype=jnp.int32),
            out(blocks * far_count, width),
            out(blocks * near_count, width),
            out(*far_coupling.shape),
            out(*left.shape),
        ),
        in_specs=[hbm] * 9 + vmem(1),
        out_specs=tuple(vmem(7)),
        scratch_shapes=[
            like(edge_field),
            like(conductance),
            like(send),
            like(panel_source),
            like(near_columns),
            like(far_columns),
            like(far_ranks),
            pltpu.VMEM((groups, width), F32),
            pltpu.SemaphoreType.DMA((9,)),
        ],
        compiler_params=PARAMS,
        cost_estimate=pl.CostEstimate(flops=10_000_000, bytes_accessed=2_500_000, transcendentals=0),
    )(
        edge_field,
        conductance,
        send,
        panel_source,
        near_columns,
        far_columns,
        far_ranks,
        far_coupling,
        left,
        side.reshape(CORES, chips + SIDE, width),
    )
    every = lax.all_gather(
        second.reshape(members * (chips + EXTRA), width),
        "group",
        axis=0,
        axis_index_groups=one_chip,
        tiled=True,
    )
    return pl.pallas_call(
        functools.partial(finish_kernel, members, chips),
        name="finish",
        out_shape=(out(*edge_field.shape), out(blocks, width)),
        in_specs=vmem(9),
        out_specs=tuple(vmem(2)),
        scratch_shapes=[
            pltpu.SMEM((8, width), jnp.int32),
            pltpu.VMEM((blocks * far_count, width), F32),
            pltpu.VMEM((blocks * near_count, width), F32),
            pltpu.SemaphoreType.DMA,
        ],
        compiler_params=PARAMS,
    )(volume, trace, index, keep, near_pick, every, near_tiles, coupling, left)


def solution(mesh):
    both = ("group", "member")
    placed = (
        P(None, "group", "member"),
        P(None, "group", "member"),
        P(both, None, None),
        P(both, None),
        P(both, None),
        P(both, None),
        P(both, None, None, None),
        P(both, None),
        P(both, None),
        P(both, None, None, None),
        P(both, None, None),
        P(both, None, None),
    )
    return jax.shard_map(
        body,
        mesh=mesh,
        in_specs=placed,
        out_specs=(P(None, "group", "member"), P(both, None)),
        check_vma=False,
    )
```

```python
import functools

import jax
import jax.numpy as jnp
from jax import lax
from jax.experimental import pallas as pl
from jax.experimental.pallas import tpu as pltpu
from jax.sharding import PartitionSpec as P

F32 = jnp.float32
BF16 = jnp.bfloat16
HIGHEST = lax.Precision.HIGHEST
CORES = 2
ROWS = 3
SIDE = 8


def split3(value):
    first = value.astype(BF16)
    rest = value - first.astype(F32)
    second = rest.astype(BF16)
    third = (rest - second.astype(F32)).astype(BF16)
    return first, second, third


def dot_exact(choice, value, dims):
    total = None
    for part in split3(value):
        term = lax.dot_general(choice, part, (dims, ((), ())), preferred_element_type=F32)
        total = term if total is None else total + term
    return total


def dot_full(left, right, dims):
    return lax.dot_general(left, right, (dims, ((), ())), precision=HIGHEST, preferred_element_type=F32)


def lanes(shape):
    return lax.broadcasted_iota(jnp.int32, shape, len(shape) - 1)


def rows(shape):
    return lax.broadcasted_iota(jnp.int32, shape, len(shape) - 2)


def upright(row, start, shape):
    wide = jnp.where(lanes(shape) == rows(shape) + start, row, 0.0)
    return jnp.sum(wide, axis=1, keepdims=True)


def fetch(pairs, sems):
    copies = [pltpu.make_async_copy(source, target, sems.at[i]) for i, (source, target) in enumerate(pairs)]
    for copy in copies:
        copy.start()
    return copies


def slot_columns(send_ref):
    slots, _, groups = send_ref.shape
    rest = jnp.zeros((8 - slots, groups), jnp.int32)
    return jnp.concatenate([send_ref[s] for s in range(slots)] + [rest], axis=0).T


def pack_kernel(
    edge_in,
    send_in,
    source_in,
    surface_in,
    right_in,
    out_ref,
    rim_ref,
    edge_ref,
    send_ref,
    source_ref,
    surface_ref,
    right_ref,
    tail_ref,
    sems,
):
    blocks, width = surface_ref.shape
    rank = right_ref.shape[1]
    height = edge_ref.shape[1]
    slots, _, groups = send_ref.shape
    chips = groups // CORES
    bits = width.bit_length() - 1
    copies = fetch(
        (
            (edge_in, edge_ref),
            (send_in, send_ref),
            (surface_in, surface_ref),
            (source_in, source_ref),
            (right_in, right_ref),
        ),
        sems,
    )
    core = lax.rem(lax.axis_index("group"), CORES)
    for copy in copies[:2]:
        copy.wait()
    for copy in copies[2:]:
        copy.wait()
    edge_x = edge_ref[0]
    edge_y = edge_ref[1]
    last_x = edge_x[height - 1 : height, :]
    beyond = jnp.where(lanes((1, width)) == width - 1, 0.0, pltpu.roll(last_x, width - 1, 1))
    down = last_x - beyond - edge_y[height - 1 : height, :]
    rim = jnp.where(core == CORES - 1, down, edge_y[0:1, :])
    own = jnp.where(core == 0, down, edge_y[0:1, :])
    next_y = jnp.where(rows((height, width)) == height - 1, 0.0, pltpu.roll(edge_y, height - 1, 0))
    flow = next_y - edge_y + edge_x
    last = (lanes((8, width)) == width - 1).astype(BF16)
    first = (lanes((8, width)) == 0).astype(BF16)
    ends = jnp.concatenate(
        [
            dot_exact(last, flow, ((1,), (1,)))[0:1, :],
            dot_exact(first, edge_x, ((1,), (1,)))[0:1, :],
            jnp.broadcast_to(edge_y[0:1, width - 1 : width], (1, width - 2 * height)),
        ],
        axis=1,
    )
    index = slot_columns(send_ref)
    parts = split3(edge_ref[...].reshape(2 * height, width))
    lane = lanes((groups, width))
    tail = jnp.where(lane == 2 * CORES * slots, last_x[0:1, 0:1], 0.0)
    for s in range(slots):
        column = jnp.broadcast_to(index[:, s : s + 1], (groups, width))
        choice = (lanes((groups, 2 * height)) == (column >> bits)[:, 0 : 2 * height]).astype(BF16)
        picked = None
        for part in parts:
            term = lax.dot_general(choice, part, (((1,), (0,)), ((), ())), preferred_element_type=F32)
            picked = term if picked is None else picked + term
        value = jnp.sum(jnp.where(lane == (column & (width - 1)), picked, 0.0), axis=1, keepdims=True)
        tail = jnp.where(lane == s, value, tail)
    slot = rows((groups, width)) * slots
    for s in range(slots):
        total = jnp.zeros((groups, width), F32)
        for b in range(blocks):
            total = total + jnp.where(source_ref[b : b + 1, :] - s == slot, surface_ref[b : b + 1, :], 0.0)
        tail = jnp.where(lane == slots + s, jnp.sum(total, axis=1, keepdims=True), tail)
    every = dot_full(surface_ref[...], right_ref[...].reshape(blocks * rank, width), ((1,), (1,)))
    mine = lanes((blocks, blocks * rank)) // rank == rows((blocks, blocks * rank))
    coeff = jnp.sum(jnp.where(mine, every, 0.0), axis=0, keepdims=True)
    out_ref[pl.ds(0, chips, stride=ROWS), :] = jnp.broadcast_to(coeff, (chips, width))
    out_ref[pl.ds(1, chips, stride=ROWS), :] = jnp.broadcast_to(rim, (chips, width))
    tail_ref[...] = tail
    even = tail_ref[pl.ds(0, chips, stride=CORES), :]
    odd = tail_ref[pl.ds(1, chips, stride=CORES), :]
    lane = lanes((chips, width))
    moved = pltpu.roll(odd, 2 * slots, 1)
    theirs = (lane >= 2 * slots) & (lane < 2 * CORES * slots)
    out_ref[pl.ds(2, chips, stride=ROWS), :] = jnp.where(theirs, moved, even)
    rim_ref[0:blocks, :] = surface_ref[...]
    rim_ref[blocks : blocks + 1, :] = ends
    rim_ref[blocks + 1 : blocks + 2, :] = own


def spread_kernel(members, slots, first_ref, rim_ref, out_ref, side_ref, block_ref):
    width = rim_ref.shape[1]
    chips = first_ref.shape[0] // ROWS
    blocks = rim_ref.shape[0] - 2
    per_member = chips + blocks + 1
    group = lax.axis_index("group")
    core = lax.rem(group, CORES)
    chip = group // CORES
    before = jnp.where(chip > 0, 1.0, 0.0)
    after = jnp.where(chip + 1 < chips, 1.0, 0.0)
    chip_before = lax.max(chip - 1, 0) * ROWS
    chip_after = lax.min(chip + 1, chips - 1) * ROWS
    rim_before = first_ref[pl.ds(chip_before + 1, 1), :] * before
    rim_after = first_ref[pl.ds(chip_after + 1, 1), :] * after
    corner_before = first_ref[pl.ds(chip_before + 2, 1), :] * before
    corners = 2 * CORES * slots
    lane = lanes((1, width))
    ends = rim_ref[blocks : blocks + 1, :]
    ends = jnp.where(lane >= 3 * width // 4, corner_before[:, corners : corners + 1], ends)
    ends = jnp.where(lane >= 7 * width // 8, rim_after[:, width - 1 : width], ends)
    block_ref[0:chips, :] = first_ref[pl.ds(0, chips, stride=ROWS), :]
    block_ref[chips : chips + blocks, :] = rim_ref[0:blocks, :]
    block_ref[chips + blocks : chips + blocks + 1, :] = ends
    for m in range(members):
        out_ref[m * per_member : (m + 1) * per_member, :] = block_ref[...]
    other = jnp.where(core == 0, rim_after, rim_before)
    side_ref[0:chips, :] = first_ref[pl.ds(2, chips, stride=ROWS), :]
    half = rows((SIDE, width)) < SIDE // 2
    side_ref[chips : chips + SIDE, :] = jnp.where(half, rim_ref[blocks + 1 : blocks + 2, :], other)


def local_kernel(
    members,
    edge_in,
    conductance_in,
    send_in,
    source_in,
    near_columns_in,
    far_columns_in,
    far_ranks_in,
    coupling_in,
    left_in,
    side_ref,
    volume_ref,
    trace_ref,
    index_ref,
    keep_ref,
    near_pick_ref,
    coupling_ref,
    left_ref,
    edge_ref,
    conductance_ref,
    send_ref,
    source_ref,
    near_columns_ref,
    far_columns_ref,
    far_ranks_ref,
    tail_ref,
    sems,
):
    copies = fetch(
        (
            (edge_in, edge_ref),
            (conductance_in, conductance_ref),
            (send_in, send_ref),
            (source_in, source_ref),
            (near_columns_in, near_columns_ref),
            (far_columns_in, far_columns_ref),
            (far_ranks_in, far_ranks_ref),
            (left_in, left_ref),
            (coupling_in, coupling_ref),
        ),
        sems,
    )
    for copy in copies[:-2]:
        copy.wait()
    blocks, width = source_ref.shape
    height = edge_ref.shape[1]
    slots, _, groups = send_ref.shape
    chips = groups // CORES
    rank = left_ref.shape[1]
    core = lax.rem(lax.axis_index("group"), CORES)
    near_count = near_columns_ref.shape[1]
    far_count = far_columns_ref.shape[1]
    column = far_columns_ref[...]
    device = column // blocks
    group = device // members
    per_member = chips + blocks + 1
    place = (group % CORES) * (members * per_member) + (device % members) * per_member + group // CORES
    rest = jnp.zeros((1, width - blocks * far_count), jnp.int32)
    index_ref[...] = jnp.concatenate([place[b : b + 1, :] for b in range(blocks)] + [rest], axis=1)
    lane = lanes((far_count, width))
    for b in range(blocks):
        square = (far_count, far_count)
        side = lanes(square) == rows(square)
        packed = column[b : b + 1, :] % blocks * width + far_ranks_ref[b : b + 1, :]
        packed = jnp.sum(jnp.where(side, packed, 0).astype(F32), axis=1, keepdims=True).astype(jnp.int32)
        kept = (lane // rank == packed // width) & (lane % rank < packed % width)
        keep_ref[b * far_count : (b + 1) * far_count, :] = kept.astype(F32)
        square = (near_count, near_count)
        side = lanes(square) == rows(square)
        picked = jnp.where(side, near_columns_ref[b : b + 1, :], 0).astype(F32)
        picked = jnp.sum(picked, axis=1, keepdims=True).astype(jnp.int32)
        near_pick_ref[b * near_count : (b + 1) * near_count, :] = (lanes((near_count, width)) == picked).astype(F32)
    for c in range(CORES):
        half = side_ref[c, 0:chips, :]
        half = jnp.where(core == 0, half, pltpu.roll(half, width - 2 * slots, 1))
        tail_ref[pl.ds(c, chips, stride=CORES), :] = half
    tail = tail_ref[...]
    slot = rows((groups, width)) * slots
    for b in range(blocks):
        trace = jnp.zeros((groups, width), F32)
        for s in range(slots):
            trace = trace + jnp.where(source_ref[b : b + 1, :] - s == slot, tail[:, s : s + 1], 0.0)
        trace_ref[b : b + 1, :] = 0.5 * jnp.sum(trace, axis=0, keepdims=True)
    index = slot_columns(send_ref)
    bits = width.bit_length() - 1
    added = None
    for s in range(slots):
        column = jnp.broadcast_to(index[:, s : s + 1], (groups, width))
        choice = (lanes((groups, 2 * height)) == (column >> bits)[:, 0 : 2 * height]).astype(BF16)
        value = jnp.where(lanes((groups, width)) == (column & (width - 1)), tail[:, slots + s : slots + s + 1], 0.0)
        term = dot_exact(choice, value, ((0,), (0,)))
        added = term if added is None else added + term
    edge_x = edge_ref[0]
    edge_y = edge_ref[1]
    shape = (height, width)
    lane = lanes(shape)
    line = rows(shape)
    own = side_ref[1 - core, chips : chips + 1, :]
    other = side_ref[1 - core, chips + SIDE // 2 : chips + SIDE // 2 + 1, :]
    above = jnp.where(core == 0, other, own)
    below = jnp.where(core == 0, own, other)
    next_x = jnp.where(lane == width - 1, 0.0, pltpu.roll(edge_x, width - 1, 1))
    next_y = jnp.where(line == height - 1, below, pltpu.roll(edge_y, height - 1, 0))
    flux = next_y - edge_y - next_x + edge_x
    flux_left = jnp.where(lane == 0, -edge_x, pltpu.roll(flux, 1, 1))
    flux_up = jnp.where(line == 0, edge_y + above, pltpu.roll(flux, 1, 0))
    volume_ref[0] = flux_left - flux + conductance_ref[0] * edge_x + added[0:height, :]
    volume_ref[1] = flux_up - flux + conductance_ref[1] * edge_y + added[height : 2 * height, :]
    for copy in copies[-2:]:
        copy.wait()


def finish_kernel(
    members,
    chips,
    volume_in,
    trace_ref,
    index_ref,
    keep_ref,
    near_pick_ref,
    every_ref,
    near_ref,
    coupling_ref,
    left_ref,
    volume_ref,
    surface_ref,
    picked_ref,
    vector_ref,
):
    blocks, width = trace_ref.shape
    height = volume_ref.shape[1]
    rank = left_ref.shape[1]
    per_member = chips + blocks + 1
    per_core = members * per_member
    core = lax.rem(lax.axis_index("group"), CORES)
    member = lax.axis_index("member")
    near_count = near_ref.shape[1]
    far_count = coupling_ref.shape[1]
    fields = [every_ref[pl.ds(core * per_core + m * per_member + chips, blocks), :] for m in range(members)]
    choice = near_pick_ref[:, 0 : members * blocks].astype(BF16)
    vector_ref[...] = dot_exact(choice, jnp.concatenate(fields, axis=0), ((1,), (0,)))
    sums = []
    for b in range(blocks):
        total = jnp.zeros((width, width), F32)
        for n in range(near_count):
            at = b * near_count + n
            total = total + near_ref[b, n] * vector_ref[at : at + 1, :]
        sums.append(total)
    near = dot_exact(jnp.ones((8, width), BF16), jnp.concatenate(sums, axis=0), ((1,), (1,)))
    for b in range(blocks):
        for f in range(far_count):
            at = b * far_count + f
            picked_ref[at : at + 1, :] = every_ref[pl.ds(index_ref[0, at], 1), :]
    picked = jnp.where(keep_ref[...] > 0.0, picked_ref[...], 0.0)
    folded = picked
    for q in range(1, width // rank):
        folded = folded + pltpu.roll(picked, q * rank, 1)
    picked_ref[...] = folded
    for b in range(blocks):
        total = jnp.zeros((rank, rank), F32)
        for f in range(far_count):
            at = b * far_count + f
            total = total + coupling_ref[b, f] * picked_ref[at : at + 1, 0:rank]
        summed = jnp.sum(total, axis=1, keepdims=True)
        far = jnp.sum(left_ref[b] * summed, axis=0, keepdims=True)
        surface_ref[b : b + 1, :] = near[0:1, b * width : (b + 1) * width] + far + trace_ref[b : b + 1, :]

    ends = chips + blocks
    before = lax.max(member - 1, 0) * per_member + ends
    after = lax.min(member + 1, members - 1) * per_member + ends
    inside = jnp.where(member > 0, 1.0, 0.0)
    mine = every_ref[pl.ds(core * per_core + before, 1), :] * inside
    theirs = every_ref[pl.ds((1 - core) * per_core + before, 1), :] * inside
    inside = jnp.where(member + 1 < members, 1.0, 0.0)
    mine_after = every_ref[pl.ds(core * per_core + after, 1), :] * inside
    theirs_after = every_ref[pl.ds((1 - core) * per_core + after, 1), :] * inside
    shape = (height, width)
    lane = lanes(shape)
    line = rows(shape)
    corner_y = 2 * height + jnp.where(core == 0, 0, 3 * height // 2)
    left = upright(mine, 0, shape)
    left = left + jnp.where(line[:, 0:1] == height - 1, upright(theirs, corner_y - height + 1, shape), 0.0)
    right = upright(mine_after, height, shape)
    corner_x = jnp.where(core == 0, 3 * height, 2 * height - 1)
    corner = jnp.sum(jnp.where(lanes((1, width)) == corner_x, theirs_after, 0.0), axis=1, keepdims=True)
    end = jnp.where(lane == width - 1, right, 0.0)
    volume_ref[0] = volume_in[0] + jnp.where(lane == 0, left, 0.0) + end
    last = jnp.where(lane == width - 1, 1.0, 0.0)
    up = jnp.where(line == 0, corner, pltpu.roll(jnp.broadcast_to(right, shape), 1, 0))
    volume_ref[1] = volume_in[1] + end - last * up


def vmem(count):
    return [pl.BlockSpec(memory_space=pltpu.VMEM)] * count


PARAMS = pltpu.CompilerParams(vmem_limit_bytes=16 * 1024 * 1024)


def body(
    edge_field,
    conductance,
    send_index,
    panel_source,
    surface_field,
    near_columns,
    near_tiles,
    far_columns,
    far_ranks,
    far_coupling,
    basis_left,
    basis_right,
):
    groups = lax.axis_size("group")
    members = lax.axis_size("member")
    slots = send_index.shape[2]
    blocks, width = surface_field.shape
    chips = groups // CORES
    per_member = chips + blocks + 1
    send = jnp.transpose(send_index, (2, 0, 1))
    right = jnp.swapaxes(basis_right, 1, 2)
    left = jnp.swapaxes(basis_left, 1, 2)
    near_count = near_columns.shape[1]
    far_count = far_columns.shape[1]
    one_core = [[chip * CORES + core for chip in range(chips)] for core in range(CORES)]
    one_chip = [[chip * CORES + core for core in range(CORES)] for chip in range(chips)]

    hbm = pl.BlockSpec(memory_space=pltpu.HBM)
    edge_field, conductance, send, panel_source, surface_field, right, left, far_coupling = [
        pltpu.with_memory_space_constraint(array, pltpu.HBM)
        for array in (edge_field, conductance, send, panel_source, surface_field, right, left, far_coupling)
    ]
    near_columns, far_columns, far_ranks = [
        pltpu.with_memory_space_constraint(array, pltpu.HBM) for array in (near_columns, far_columns, far_ranks)
    ]

    def like(array):
        return pltpu.VMEM(array.shape, array.dtype)

    def out(*shape, dtype=F32):
        return jax.ShapeDtypeStruct(shape, dtype)

    first, rim = pl.pallas_call(
        pack_kernel,
        name="pack",
        out_shape=(out(chips * ROWS, width), out(blocks + 2, width)),
        in_specs=[hbm] * 5,
        out_specs=tuple(vmem(2)),
        scratch_shapes=[
            like(edge_field),
            like(send),
            like(panel_source),
            like(surface_field),
            like(right),
            pltpu.VMEM((groups, width), F32),
            pltpu.SemaphoreType.DMA((5,)),
        ],
        compiler_params=PARAMS,
    )(edge_field, send, panel_source, surface_field, right)
    first = lax.all_to_all(
        first.reshape(chips, 1, ROWS * width),
        "group",
        split_axis=0,
        concat_axis=0,
        axis_index_groups=one_core,
        tiled=True,
    ).reshape(chips * ROWS, width)
    second, side = pl.pallas_call(
        functools.partial(spread_kernel, members, slots),
        name="spread",
        out_shape=(out(members * per_member, width), out(chips + SIDE, width)),
        in_specs=vmem(2),
        out_specs=tuple(vmem(2)),
        scratch_shapes=[pltpu.VMEM((per_member, width), F32)],
        compiler_params=PARAMS,
    )(first, rim)
    second = lax.all_to_all(
        second.reshape(members, 1, per_member * width), "member", split_axis=0, concat_axis=0, tiled=True
    )
    side = lax.all_gather(side, "group", axis=0, axis_index_groups=one_chip, tiled=True)
    volume, trace, index, keep, near_pick, coupling, left = pl.pallas_call(
        functools.partial(local_kernel, members),
        name="local",
        out_shape=(
            out(*edge_field.shape),
            out(blocks, width),
            out(1, width, dtype=jnp.int32),
            out(blocks * far_count, width),
            out(blocks * near_count, width),
            out(*far_coupling.shape),
            out(*left.shape),
        ),
        in_specs=[hbm] * 9 + vmem(1),
        out_specs=tuple(vmem(7)),
        scratch_shapes=[
            like(edge_field),
            like(conductance),
            like(send),
            like(panel_source),
            like(near_columns),
            like(far_columns),
            like(far_ranks),
            pltpu.VMEM((groups, width), F32),
            pltpu.SemaphoreType.DMA((9,)),
        ],
        compiler_params=PARAMS,
        cost_estimate=pl.CostEstimate(flops=10_000_000, bytes_accessed=2_500_000, transcendentals=0),
    )(
        edge_field,
        conductance,
        send,
        panel_source,
        near_columns,
        far_columns,
        far_ranks,
        far_coupling,
        left,
        side.reshape(CORES, chips + SIDE, width),
    )
    every = lax.all_gather(
        second.reshape(members * per_member, width),
        "group",
        axis=0,
        axis_index_groups=one_chip,
        tiled=True,
    )
    return pl.pallas_call(
        functools.partial(finish_kernel, members, chips),
        name="finish",
        out_shape=(out(*edge_field.shape), out(blocks, width)),
        in_specs=vmem(9),
        out_specs=tuple(vmem(2)),
        scratch_shapes=[
            pltpu.VMEM((blocks * far_count, width), F32),
            pltpu.VMEM((blocks * near_count, width), F32),
        ],
        compiler_params=PARAMS,
    )(volume, trace, index, keep, near_pick, every, near_tiles, coupling, left)


def solution(mesh):
    both = ("group", "member")
    placed = (
        P(None, "group", "member"),
        P(None, "group", "member"),
        P(both, None, None),
        P(both, None),
        P(both, None),
        P(both, None),
        P(both, None, None, None),
        P(both, None),
        P(both, None),
        P(both, None, None, None),
        P(both, None, None),
        P(both, None, None),
    )
    return jax.shard_map(
        body,
        mesh=mesh,
        in_specs=placed,
        out_specs=(P(None, "group", "member"), P(both, None)),
        check_vma=False,
    )
```

```python
import functools

import jax
import jax.numpy as jnp
from jax import lax
from jax.experimental import pallas as pl
from jax.experimental.pallas import tpu as pltpu
from jax.sharding import PartitionSpec as P

F32 = jnp.float32
BF16 = jnp.bfloat16
HIGHEST = lax.Precision.HIGHEST
CORES = 2
ROWS = 3
SIDE = 8


def split3(value):
    first = value.astype(BF16)
    rest = value - first.astype(F32)
    second = rest.astype(BF16)
    third = (rest - second.astype(F32)).astype(BF16)
    return first, second, third


def dot_exact(choice, value, dims):
    total = None
    for part in split3(value):
        term = lax.dot_general(choice, part, (dims, ((), ())), preferred_element_type=F32)
        total = term if total is None else total + term
    return total


def dot_full(left, right, dims):
    return lax.dot_general(left, right, (dims, ((), ())), precision=HIGHEST, preferred_element_type=F32)


def lanes(shape):
    return lax.broadcasted_iota(jnp.int32, shape, len(shape) - 1)


def rows(shape):
    return lax.broadcasted_iota(jnp.int32, shape, len(shape) - 2)


def upright(row, start, shape):
    wide = jnp.where(lanes(shape) == rows(shape) + start, row, 0.0)
    return jnp.sum(wide, axis=1, keepdims=True)


def side_of(member, members):
    return 2 * member // members


def fetch(pairs, sems):
    copies = [pltpu.make_async_copy(source, target, sems.at[i]) for i, (source, target) in enumerate(pairs)]
    for copy in copies:
        copy.start()
    return copies


def slot_columns(send_ref):
    slots, _, groups = send_ref.shape
    rest = jnp.zeros((8 - slots, groups), jnp.int32)
    return jnp.concatenate([send_ref[s] for s in range(slots)] + [rest], axis=0).T


def pack_kernel(
    edge_in,
    send_in,
    source_in,
    surface_in,
    right_in,
    out_ref,
    rim_ref,
    edge_ref,
    send_ref,
    source_ref,
    surface_ref,
    right_ref,
    tail_ref,
    sems,
):
    blocks, width = surface_ref.shape
    rank = right_ref.shape[1]
    height = edge_ref.shape[1]
    slots, _, groups = send_ref.shape
    chips = groups // CORES
    bits = width.bit_length() - 1
    copies = fetch(
        (
            (edge_in, edge_ref),
            (send_in, send_ref),
            (surface_in, surface_ref),
            (source_in, source_ref),
            (right_in, right_ref),
        ),
        sems,
    )
    core = lax.rem(lax.axis_index("group"), CORES)
    for copy in copies[:2]:
        copy.wait()
    for copy in copies[2:]:
        copy.wait()
    edge_x = edge_ref[0]
    edge_y = edge_ref[1]
    last_x = edge_x[height - 1 : height, :]
    beyond = jnp.where(lanes((1, width)) == width - 1, 0.0, pltpu.roll(last_x, width - 1, 1))
    down = last_x - beyond - edge_y[height - 1 : height, :]
    rim = jnp.where(core == CORES - 1, down, edge_y[0:1, :])
    own = jnp.where(core == 0, down, edge_y[0:1, :])
    next_y = jnp.where(rows((height, width)) == height - 1, 0.0, pltpu.roll(edge_y, height - 1, 0))
    flow = next_y - edge_y + edge_x
    last = (lanes((8, width)) == width - 1).astype(BF16)
    first = (lanes((8, width)) == 0).astype(BF16)
    ends = jnp.concatenate(
        [
            dot_exact(last, flow, ((1,), (1,)))[0:1, :],
            dot_exact(first, edge_x, ((1,), (1,)))[0:1, :],
            jnp.broadcast_to(edge_y[0:1, width - 1 : width], (1, width - 2 * height)),
        ],
        axis=1,
    )
    index = slot_columns(send_ref)
    parts = split3(edge_ref[...].reshape(2 * height, width))
    lane = lanes((groups, width))
    tail = jnp.where(lane == 2 * CORES * slots, last_x[0:1, 0:1], 0.0)
    for s in range(slots):
        column = jnp.broadcast_to(index[:, s : s + 1], (groups, width))
        choice = (lanes((groups, 2 * height)) == (column >> bits)[:, 0 : 2 * height]).astype(BF16)
        picked = None
        for part in parts:
            term = lax.dot_general(choice, part, (((1,), (0,)), ((), ())), preferred_element_type=F32)
            picked = term if picked is None else picked + term
        value = jnp.sum(jnp.where(lane == (column & (width - 1)), picked, 0.0), axis=1, keepdims=True)
        tail = jnp.where(lane == s, value, tail)
    slot = rows((groups, width)) * slots
    for s in range(slots):
        total = jnp.zeros((groups, width), F32)
        for b in range(blocks):
            total = total + jnp.where(source_ref[b : b + 1, :] - s == slot, surface_ref[b : b + 1, :], 0.0)
        tail = jnp.where(lane == slots + s, jnp.sum(total, axis=1, keepdims=True), tail)
    every = dot_full(surface_ref[...], right_ref[...].reshape(blocks * rank, width), ((1,), (1,)))
    mine = lanes((blocks, blocks * rank)) // rank == rows((blocks, blocks * rank))
    coeff = jnp.sum(jnp.where(mine, every, 0.0), axis=0, keepdims=True)
    out_ref[pl.ds(0, chips, stride=ROWS), :] = jnp.broadcast_to(coeff, (chips, width))
    out_ref[pl.ds(1, chips, stride=ROWS), :] = jnp.broadcast_to(rim, (chips, width))
    tail_ref[...] = tail
    even = tail_ref[pl.ds(0, chips, stride=CORES), :]
    odd = tail_ref[pl.ds(1, chips, stride=CORES), :]
    lane = lanes((chips, width))
    moved = pltpu.roll(odd, 2 * slots, 1)
    theirs = (lane >= 2 * slots) & (lane < 2 * CORES * slots)
    out_ref[pl.ds(2, chips, stride=ROWS), :] = jnp.where(theirs, moved, even)
    rim_ref[0:blocks, :] = surface_ref[...]
    rim_ref[blocks : blocks + 1, :] = ends
    rim_ref[blocks + 1 : blocks + 2, :] = own


def spread_kernel(members, slots, first_ref, rim_ref, out_ref, side_ref, block_ref):
    width = rim_ref.shape[1]
    chips = first_ref.shape[0] // ROWS
    blocks = rim_ref.shape[0] - 2
    per_member = chips + blocks + 1
    group = lax.axis_index("group")
    core = lax.rem(group, CORES)
    chip = group // CORES
    before = jnp.where(chip > 0, 1.0, 0.0)
    after = jnp.where(chip + 1 < chips, 1.0, 0.0)
    chip_before = lax.max(chip - 1, 0) * ROWS
    chip_after = lax.min(chip + 1, chips - 1) * ROWS
    rim_before = first_ref[pl.ds(chip_before + 1, 1), :] * before
    rim_after = first_ref[pl.ds(chip_after + 1, 1), :] * after
    corner_before = first_ref[pl.ds(chip_before + 2, 1), :] * before
    corners = 2 * CORES * slots
    lane = lanes((1, width))
    ends = rim_ref[blocks : blocks + 1, :]
    ends = jnp.where(lane >= 3 * width // 4, corner_before[:, corners : corners + 1], ends)
    ends = jnp.where(lane >= 7 * width // 8, rim_after[:, width - 1 : width], ends)
    block_ref[0:chips, :] = first_ref[pl.ds(0, chips, stride=ROWS), :]
    block_ref[chips : chips + blocks, :] = rim_ref[0:blocks, :]
    block_ref[chips + blocks : chips + blocks + 1, :] = ends
    for m in range(members):
        out_ref[m * per_member : (m + 1) * per_member, :] = block_ref[...]
    other = jnp.where(core == 0, rim_after, rim_before)
    side_ref[0:chips, :] = first_ref[pl.ds(2, chips, stride=ROWS), :]
    half = rows((SIDE, width)) < SIDE // 2
    side_ref[chips : chips + SIDE, :] = jnp.where(half, rim_ref[blocks + 1 : blocks + 2, :], other)


def local_kernel(
    members,
    edge_in,
    conductance_in,
    send_in,
    source_in,
    near_columns_in,
    far_columns_in,
    far_ranks_in,
    coupling_in,
    left_in,
    side_ref,
    volume_ref,
    trace_ref,
    index_ref,
    keep_ref,
    near_pick_ref,
    coupling_ref,
    left_ref,
    edge_ref,
    conductance_ref,
    send_ref,
    source_ref,
    near_columns_ref,
    far_columns_ref,
    far_ranks_ref,
    tail_ref,
    sems,
):
    copies = fetch(
        (
            (edge_in, edge_ref),
            (conductance_in, conductance_ref),
            (send_in, send_ref),
            (source_in, source_ref),
            (near_columns_in, near_columns_ref),
            (far_columns_in, far_columns_ref),
            (far_ranks_in, far_ranks_ref),
            (left_in, left_ref),
            (coupling_in, coupling_ref),
        ),
        sems,
    )
    for copy in copies[:-2]:
        copy.wait()
    blocks, width = source_ref.shape
    height = edge_ref.shape[1]
    slots, _, groups = send_ref.shape
    chips = groups // CORES
    rank = left_ref.shape[1]
    core = lax.rem(lax.axis_index("group"), CORES)
    near_count = near_columns_ref.shape[1]
    far_count = far_columns_ref.shape[1]
    column = far_columns_ref[...]
    device = column // blocks
    group = device // members
    per_member = chips + blocks + 1
    owner = device % members
    here = side_of(lax.axis_index("member"), members)
    held = (group + side_of(owner, members) + here) % CORES
    place = held * (members * per_member) + owner * per_member + group // CORES
    rest = jnp.zeros((1, width - blocks * far_count), jnp.int32)
    index_ref[...] = jnp.concatenate([place[b : b + 1, :] for b in range(blocks)] + [rest], axis=1)
    lane = lanes((far_count, width))
    for b in range(blocks):
        square = (far_count, far_count)
        side = lanes(square) == rows(square)
        packed = column[b : b + 1, :] % blocks * width + far_ranks_ref[b : b + 1, :]
        packed = jnp.sum(jnp.where(side, packed, 0).astype(F32), axis=1, keepdims=True).astype(jnp.int32)
        kept = (lane // rank == packed // width) & (lane % rank < packed % width)
        keep_ref[b * far_count : (b + 1) * far_count, :] = kept.astype(F32)
        square = (near_count, near_count)
        side = lanes(square) == rows(square)
        picked = jnp.where(side, near_columns_ref[b : b + 1, :], 0).astype(F32)
        picked = jnp.sum(picked, axis=1, keepdims=True).astype(jnp.int32)
        near_pick_ref[b * near_count : (b + 1) * near_count, :] = (lanes((near_count, width)) == picked).astype(F32)
    for c in range(CORES):
        half = side_ref[c, 0:chips, :]
        half = jnp.where(core == 0, half, pltpu.roll(half, width - 2 * slots, 1))
        tail_ref[pl.ds(c, chips, stride=CORES), :] = half
    tail = tail_ref[...]
    slot = rows((groups, width)) * slots
    for b in range(blocks):
        trace = jnp.zeros((groups, width), F32)
        for s in range(slots):
            trace = trace + jnp.where(source_ref[b : b + 1, :] - s == slot, tail[:, s : s + 1], 0.0)
        trace_ref[b : b + 1, :] = 0.5 * jnp.sum(trace, axis=0, keepdims=True)
    index = slot_columns(send_ref)
    bits = width.bit_length() - 1
    added = None
    for s in range(slots):
        column = jnp.broadcast_to(index[:, s : s + 1], (groups, width))
        choice = (lanes((groups, 2 * height)) == (column >> bits)[:, 0 : 2 * height]).astype(BF16)
        value = jnp.where(lanes((groups, width)) == (column & (width - 1)), tail[:, slots + s : slots + s + 1], 0.0)
        term = dot_exact(choice, value, ((0,), (0,)))
        added = term if added is None else added + term
    edge_x = edge_ref[0]
    edge_y = edge_ref[1]
    shape = (height, width)
    lane = lanes(shape)
    line = rows(shape)
    own = side_ref[1 - core, chips : chips + 1, :]
    other = side_ref[1 - core, chips + SIDE // 2 : chips + SIDE // 2 + 1, :]
    above = jnp.where(core == 0, other, own)
    below = jnp.where(core == 0, own, other)
    next_x = jnp.where(lane == width - 1, 0.0, pltpu.roll(edge_x, width - 1, 1))
    next_y = jnp.where(line == height - 1, below, pltpu.roll(edge_y, height - 1, 0))
    flux = next_y - edge_y - next_x + edge_x
    flux_left = jnp.where(lane == 0, -edge_x, pltpu.roll(flux, 1, 1))
    flux_up = jnp.where(line == 0, edge_y + above, pltpu.roll(flux, 1, 0))
    volume_ref[0] = flux_left - flux + conductance_ref[0] * edge_x + added[0:height, :]
    volume_ref[1] = flux_up - flux + conductance_ref[1] * edge_y + added[height : 2 * height, :]
    for copy in copies[-2:]:
        copy.wait()


def finish_kernel(
    members,
    chips,
    volume_in,
    trace_ref,
    index_ref,
    keep_ref,
    near_pick_ref,
    every_ref,
    near_ref,
    coupling_ref,
    left_ref,
    volume_ref,
    surface_ref,
    picked_ref,
    vector_ref,
):
    blocks, width = trace_ref.shape
    height = volume_ref.shape[1]
    rank = left_ref.shape[1]
    per_member = chips + blocks + 1
    per_core = members * per_member
    core = lax.rem(lax.axis_index("group"), CORES)
    member = lax.axis_index("member")
    near_count = near_ref.shape[1]
    far_count = coupling_ref.shape[1]
    here = side_of(member, members)
    fields = []
    for m in range(members):
        held = lax.rem(core + side_of(m, members) + here, CORES)
        fields.append(every_ref[pl.ds(held * per_core + m * per_member + chips, blocks), :])
    choice = near_pick_ref[:, 0 : members * blocks].astype(BF16)
    vector_ref[...] = dot_exact(choice, jnp.concatenate(fields, axis=0), ((1,), (0,)))
    sums = []
    for b in range(blocks):
        total = jnp.zeros((width, width), F32)
        for n in range(near_count):
            at = b * near_count + n
            total = total + near_ref[b, n] * vector_ref[at : at + 1, :]
        sums.append(total)
    near = dot_exact(jnp.ones((8, width), BF16), jnp.concatenate(sums, axis=0), ((1,), (1,)))
    for b in range(blocks):
        for f in range(far_count):
            at = b * far_count + f
            picked_ref[at : at + 1, :] = every_ref[pl.ds(index_ref[0, at], 1), :]
    picked = jnp.where(keep_ref[...] > 0.0, picked_ref[...], 0.0)
    folded = picked
    for q in range(1, width // rank):
        folded = folded + pltpu.roll(picked, q * rank, 1)
    picked_ref[...] = folded
    for b in range(blocks):
        total = jnp.zeros((rank, rank), F32)
        for f in range(far_count):
            at = b * far_count + f
            total = total + coupling_ref[b, f] * picked_ref[at : at + 1, 0:rank]
        summed = jnp.sum(total, axis=1, keepdims=True)
        far = jnp.sum(left_ref[b] * summed, axis=0, keepdims=True)
        surface_ref[b : b + 1, :] = near[0:1, b * width : (b + 1) * width] + far + trace_ref[b : b + 1, :]

    ends = chips + blocks

    def rim_of(other):
        inside = jnp.where((other >= 0) & (other < members), 1.0, 0.0)
        other = lax.clamp(0, other, members - 1)
        held = lax.rem(core + side_of(other, members) + here, CORES)
        row = other * per_member + ends
        mine = every_ref[pl.ds(held * per_core + row, 1), :] * inside
        theirs = every_ref[pl.ds((1 - held) * per_core + row, 1), :] * inside
        return mine, theirs

    mine, theirs = rim_of(member - 1)
    mine_after, theirs_after = rim_of(member + 1)
    shape = (height, width)
    lane = lanes(shape)
    line = rows(shape)
    corner_y = 2 * height + jnp.where(core == 0, 0, 3 * height // 2)
    left = upright(mine, 0, shape)
    left = left + jnp.where(line[:, 0:1] == height - 1, upright(theirs, corner_y - height + 1, shape), 0.0)
    right = upright(mine_after, height, shape)
    corner_x = jnp.where(core == 0, 3 * height, 2 * height - 1)
    corner = jnp.sum(jnp.where(lanes((1, width)) == corner_x, theirs_after, 0.0), axis=1, keepdims=True)
    end = jnp.where(lane == width - 1, right, 0.0)
    volume_ref[0] = volume_in[0] + jnp.where(lane == 0, left, 0.0) + end
    last = jnp.where(lane == width - 1, 1.0, 0.0)
    up = jnp.where(line == 0, corner, pltpu.roll(jnp.broadcast_to(right, shape), 1, 0))
    volume_ref[1] = volume_in[1] + end - last * up


def vmem(count):
    return [pl.BlockSpec(memory_space=pltpu.VMEM)] * count


PARAMS = pltpu.CompilerParams(vmem_limit_bytes=16 * 1024 * 1024)


def body(
    edge_field,
    conductance,
    send_index,
    panel_source,
    surface_field,
    near_columns,
    near_tiles,
    far_columns,
    far_ranks,
    far_coupling,
    basis_left,
    basis_right,
):
    groups = lax.axis_size("group")
    members = lax.axis_size("member")
    slots = send_index.shape[2]
    blocks, width = surface_field.shape
    chips = groups // CORES
    per_member = chips + blocks + 1
    send = jnp.transpose(send_index, (2, 0, 1))
    right = jnp.swapaxes(basis_right, 1, 2)
    left = jnp.swapaxes(basis_left, 1, 2)
    near_count = near_columns.shape[1]
    far_count = far_columns.shape[1]
    one_core = [[chip * CORES + core for chip in range(chips)] for core in range(CORES)]
    crossed = [
        [(chip * CORES + (core + side_of(m, members)) % CORES) * members + m for m in range(members)]
        for chip in range(chips)
        for core in range(CORES)
    ]
    one_chip = [[chip * CORES + core for core in range(CORES)] for chip in range(chips)]

    hbm = pl.BlockSpec(memory_space=pltpu.HBM)
    edge_field, conductance, send, panel_source, surface_field, right, left, far_coupling = [
        pltpu.with_memory_space_constraint(array, pltpu.HBM)
        for array in (edge_field, conductance, send, panel_source, surface_field, right, left, far_coupling)
    ]
    near_columns, far_columns, far_ranks = [
        pltpu.with_memory_space_constraint(array, pltpu.HBM) for array in (near_columns, far_columns, far_ranks)
    ]

    def like(array):
        return pltpu.VMEM(array.shape, array.dtype)

    def out(*shape, dtype=F32):
        return jax.ShapeDtypeStruct(shape, dtype)

    first, rim = pl.pallas_call(
        pack_kernel,
        name="pack",
        out_shape=(out(chips * ROWS, width), out(blocks + 2, width)),
        in_specs=[hbm] * 5,
        out_specs=tuple(vmem(2)),
        scratch_shapes=[
            like(edge_field),
            like(send),
            like(panel_source),
            like(surface_field),
            like(right),
            pltpu.VMEM((groups, width), F32),
            pltpu.SemaphoreType.DMA((5,)),
        ],
        compiler_params=PARAMS,
    )(edge_field, send, panel_source, surface_field, right)
    first = lax.all_to_all(
        first.reshape(chips, 1, ROWS * width),
        "group",
        split_axis=0,
        concat_axis=0,
        axis_index_groups=one_core,
        tiled=True,
    ).reshape(chips * ROWS, width)
    second, side = pl.pallas_call(
        functools.partial(spread_kernel, members, slots),
        name="spread",
        out_shape=(out(members * per_member, width), out(chips + SIDE, width)),
        in_specs=vmem(2),
        out_specs=tuple(vmem(2)),
        scratch_shapes=[pltpu.VMEM((per_member, width), F32)],
        compiler_params=PARAMS,
    )(first, rim)
    second = lax.all_to_all(
        second.reshape(members, 1, per_member * width),
        ("group", "member"),
        split_axis=0,
        concat_axis=0,
        axis_index_groups=crossed,
        tiled=True,
    )
    side = lax.all_gather(side, "group", axis=0, axis_index_groups=one_chip, tiled=True)
    volume, trace, index, keep, near_pick, coupling, left = pl.pallas_call(
        functools.partial(local_kernel, members),
        name="local",
        out_shape=(
            out(*edge_field.shape),
            out(blocks, width),
            out(1, width, dtype=jnp.int32),
            out(blocks * far_count, width),
            out(blocks * near_count, width),
            out(*far_coupling.shape),
            out(*left.shape),
        ),
        in_specs=[hbm] * 9 + vmem(1),
        out_specs=tuple(vmem(7)),
        scratch_shapes=[
            like(edge_field),
            like(conductance),
            like(send),
            like(panel_source),
            like(near_columns),
            like(far_columns),
            like(far_ranks),
            pltpu.VMEM((groups, width), F32),
            pltpu.SemaphoreType.DMA((9,)),
        ],
        compiler_params=PARAMS,
        cost_estimate=pl.CostEstimate(flops=10_000_000, bytes_accessed=2_500_000, transcendentals=0),
    )(
        edge_field,
        conductance,
        send,
        panel_source,
        near_columns,
        far_columns,
        far_ranks,
        far_coupling,
        left,
        side.reshape(CORES, chips + SIDE, width),
    )
    every = lax.all_gather(
        second.reshape(members * per_member, width),
        "group",
        axis=0,
        axis_index_groups=one_chip,
        tiled=True,
    )
    return pl.pallas_call(
        functools.partial(finish_kernel, members, chips),
        name="finish",
        out_shape=(out(*edge_field.shape), out(blocks, width)),
        in_specs=vmem(9),
        out_specs=tuple(vmem(2)),
        scratch_shapes=[
            pltpu.VMEM((blocks * far_count, width), F32),
            pltpu.VMEM((blocks * near_count, width), F32),
        ],
        compiler_params=PARAMS,
    )(volume, trace, index, keep, near_pick, every, near_tiles, coupling, left)


def solution(mesh):
    both = ("group", "member")
    placed = (
        P(None, "group", "member"),
        P(None, "group", "member"),
        P(both, None, None),
        P(both, None),
        P(both, None),
        P(both, None),
        P(both, None, None, None),
        P(both, None),
        P(both, None),
        P(both, None, None, None),
        P(both, None, None),
        P(both, None, None),
    )
    return jax.shard_map(
        body,
        mesh=mesh,
        in_specs=placed,
        out_specs=(P(None, "group", "member"), P(both, None)),
        check_vma=False,
    )
```

```python
import functools

import jax
import jax.numpy as jnp
from jax import lax
from jax.experimental import pallas as pl
from jax.experimental.pallas import tpu as pltpu
from jax.sharding import PartitionSpec as P

F32 = jnp.float32
BF16 = jnp.bfloat16
HIGHEST = lax.Precision.HIGHEST
FIRST_CHIP = 38
FIRST_MEMBER = 4
CORES = 2
ROWS = 3
SIDE = 8


def split3(value):
    first = value.astype(BF16)
    rest = value - first.astype(F32)
    second = rest.astype(BF16)
    third = (rest - second.astype(F32)).astype(BF16)
    return first, second, third


def dot_exact(choice, value, dims):
    total = None
    for part in split3(value):
        term = lax.dot_general(choice, part, (dims, ((), ())), preferred_element_type=F32)
        total = term if total is None else total + term
    return total


def dot_full(left, right, dims):
    return lax.dot_general(left, right, (dims, ((), ())), precision=HIGHEST, preferred_element_type=F32)


def lanes(shape):
    return lax.broadcasted_iota(jnp.int32, shape, len(shape) - 1)


def rows(shape):
    return lax.broadcasted_iota(jnp.int32, shape, len(shape) - 2)


def upright(row, start, shape):
    wide = jnp.where(lanes(shape) == rows(shape) + start, row, 0.0)
    return jnp.sum(wide, axis=1, keepdims=True)


def spot(index, first, count):
    return (index + (count - first % count)) % count


def side_of(member, members):
    return 2 * member // members


def fetch(pairs, sems):
    copies = [pltpu.make_async_copy(source, target, sems.at[i]) for i, (source, target) in enumerate(pairs)]
    for copy in copies:
        copy.start()
    return copies


def slot_columns(send_ref):
    slots, _, groups = send_ref.shape
    rest = jnp.zeros((8 - slots, groups), jnp.int32)
    return jnp.concatenate([send_ref[s] for s in range(slots)] + [rest], axis=0).T


def pack_kernel(
    edge_in,
    send_in,
    source_in,
    surface_in,
    right_in,
    out_ref,
    rim_ref,
    edge_ref,
    send_ref,
    source_ref,
    surface_ref,
    right_ref,
    tail_ref,
    sems,
):
    blocks, width = surface_ref.shape
    rank = right_ref.shape[1]
    height = edge_ref.shape[1]
    slots, _, groups = send_ref.shape
    chips = groups // CORES
    bits = width.bit_length() - 1
    copies = fetch(
        (
            (edge_in, edge_ref),
            (send_in, send_ref),
            (surface_in, surface_ref),
            (source_in, source_ref),
            (right_in, right_ref),
        ),
        sems,
    )
    core = lax.rem(lax.axis_index("group"), CORES)
    for copy in copies[:2]:
        copy.wait()
    for copy in copies[2:]:
        copy.wait()
    edge_x = edge_ref[0]
    edge_y = edge_ref[1]
    last_x = edge_x[height - 1 : height, :]
    beyond = jnp.where(lanes((1, width)) == width - 1, 0.0, pltpu.roll(last_x, width - 1, 1))
    down = last_x - beyond - edge_y[height - 1 : height, :]
    rim = jnp.where(core == CORES - 1, down, edge_y[0:1, :])
    own = jnp.where(core == 0, down, edge_y[0:1, :])
    next_y = jnp.where(rows((height, width)) == height - 1, 0.0, pltpu.roll(edge_y, height - 1, 0))
    flow = next_y - edge_y + edge_x
    last = (lanes((8, width)) == width - 1).astype(BF16)
    first = (lanes((8, width)) == 0).astype(BF16)
    ends = jnp.concatenate(
        [
            dot_exact(last, flow, ((1,), (1,)))[0:1, :],
            dot_exact(first, edge_x, ((1,), (1,)))[0:1, :],
            jnp.broadcast_to(edge_y[0:1, width - 1 : width], (1, width - 2 * height)),
        ],
        axis=1,
    )
    index = slot_columns(send_ref)
    parts = split3(edge_ref[...].reshape(2 * height, width))
    lane = lanes((groups, width))
    tail = jnp.where(lane == 2 * CORES * slots, last_x[0:1, 0:1], 0.0)
    for s in range(slots):
        column = jnp.broadcast_to(index[:, s : s + 1], (groups, width))
        choice = (lanes((groups, 2 * height)) == (column >> bits)[:, 0 : 2 * height]).astype(BF16)
        picked = None
        for part in parts:
            term = lax.dot_general(choice, part, (((1,), (0,)), ((), ())), preferred_element_type=F32)
            picked = term if picked is None else picked + term
        value = jnp.sum(jnp.where(lane == (column & (width - 1)), picked, 0.0), axis=1, keepdims=True)
        tail = jnp.where(lane == s, value, tail)
    slot = rows((groups, width)) * slots
    for s in range(slots):
        total = jnp.zeros((groups, width), F32)
        for b in range(blocks):
            total = total + jnp.where(source_ref[b : b + 1, :] - s == slot, surface_ref[b : b + 1, :], 0.0)
        tail = jnp.where(lane == slots + s, jnp.sum(total, axis=1, keepdims=True), tail)
    every = dot_full(surface_ref[...], right_ref[...].reshape(blocks * rank, width), ((1,), (1,)))
    mine = lanes((blocks, blocks * rank)) // rank == rows((blocks, blocks * rank))
    coeff = jnp.sum(jnp.where(mine, every, 0.0), axis=0, keepdims=True)
    out_ref[pl.ds(0, chips, stride=ROWS), :] = jnp.broadcast_to(coeff, (chips, width))
    out_ref[pl.ds(1, chips, stride=ROWS), :] = jnp.broadcast_to(rim, (chips, width))
    tail_ref[...] = tail
    lane = lanes((chips, width))
    even = tail_ref[pl.ds(0, chips, stride=CORES), :]
    odd = tail_ref[pl.ds(1, chips, stride=CORES), :]
    moved = pltpu.roll(odd, 2 * slots, 1)
    theirs = (lane >= 2 * slots) & (lane < 2 * CORES * slots)
    both = jnp.where(theirs, moved, even)
    turn = FIRST_CHIP % chips
    out_ref[pl.ds(2, chips - turn, stride=ROWS), :] = both[turn:, :]
    out_ref[pl.ds(2 + ROWS * (chips - turn), turn, stride=ROWS), :] = both[:turn, :]
    rim_ref[0:blocks, :] = surface_ref[...]
    rim_ref[blocks : blocks + 1, :] = ends
    rim_ref[blocks + 1 : blocks + 2, :] = own


def spread_kernel(members, slots, first_ref, rim_ref, out_ref, side_ref, block_ref):
    width = rim_ref.shape[1]
    chips = first_ref.shape[0] // ROWS
    blocks = rim_ref.shape[0] - 2
    per_member = chips + blocks + 1
    group = lax.axis_index("group")
    core = lax.rem(group, CORES)
    chip = group // CORES
    before = jnp.where(chip > 0, 1.0, 0.0)
    after = jnp.where(chip + 1 < chips, 1.0, 0.0)
    chip_before = spot(lax.max(chip - 1, 0), FIRST_CHIP, chips) * ROWS
    chip_after = spot(lax.min(chip + 1, chips - 1), FIRST_CHIP, chips) * ROWS
    rim_before = first_ref[pl.ds(chip_before + 1, 1), :] * before
    rim_after = first_ref[pl.ds(chip_after + 1, 1), :] * after
    corner_before = first_ref[pl.ds(chip_before + 2, 1), :] * before
    corners = 2 * CORES * slots
    lane = lanes((1, width))
    ends = rim_ref[blocks : blocks + 1, :]
    ends = jnp.where(lane >= 3 * width // 4, corner_before[:, corners : corners + 1], ends)
    ends = jnp.where(lane >= 7 * width // 8, rim_after[:, width - 1 : width], ends)
    block_ref[0:chips, :] = first_ref[pl.ds(0, chips, stride=ROWS), :]
    block_ref[chips : chips + blocks, :] = rim_ref[0:blocks, :]
    block_ref[chips + blocks : chips + blocks + 1, :] = ends
    for m in range(members):
        out_ref[m * per_member : (m + 1) * per_member, :] = block_ref[...]
    other = jnp.where(core == 0, rim_after, rim_before)
    side_ref[0:chips, :] = first_ref[pl.ds(2, chips, stride=ROWS), :]
    half = rows((SIDE, width)) < SIDE // 2
    side_ref[chips : chips + SIDE, :] = jnp.where(half, rim_ref[blocks + 1 : blocks + 2, :], other)


def local_kernel(
    members,
    edge_in,
    conductance_in,
    send_in,
    source_in,
    near_columns_in,
    far_columns_in,
    far_ranks_in,
    coupling_in,
    left_in,
    side_ref,
    volume_ref,
    trace_ref,
    index_ref,
    keep_ref,
    near_pick_ref,
    coupling_ref,
    left_ref,
    edge_ref,
    conductance_ref,
    send_ref,
    source_ref,
    near_columns_ref,
    far_columns_ref,
    far_ranks_ref,
    tail_ref,
    sems,
):
    copies = fetch(
        (
            (edge_in, edge_ref),
            (conductance_in, conductance_ref),
            (send_in, send_ref),
            (source_in, source_ref),
            (near_columns_in, near_columns_ref),
            (far_columns_in, far_columns_ref),
            (far_ranks_in, far_ranks_ref),
            (left_in, left_ref),
            (coupling_in, coupling_ref),
        ),
        sems,
    )
    for copy in copies[:-2]:
        copy.wait()
    blocks, width = source_ref.shape
    height = edge_ref.shape[1]
    slots, _, groups = send_ref.shape
    chips = groups // CORES
    rank = left_ref.shape[1]
    core = lax.rem(lax.axis_index("group"), CORES)
    near_count = near_columns_ref.shape[1]
    far_count = far_columns_ref.shape[1]
    column = far_columns_ref[...]
    device = column // blocks
    group = device // members
    per_member = chips + blocks + 1
    owner = device % members
    here = side_of(lax.axis_index("member"), members)
    held = (group + side_of(owner, members) + here) % CORES
    owner = spot(owner, FIRST_MEMBER, members)
    place = held * (members * per_member) + owner * per_member + spot(group // CORES, FIRST_CHIP, chips)
    rest = jnp.zeros((1, width - blocks * far_count), jnp.int32)
    index_ref[...] = jnp.concatenate([place[b : b + 1, :] for b in range(blocks)] + [rest], axis=1)
    lane = lanes((far_count, width))
    for b in range(blocks):
        square = (far_count, far_count)
        side = lanes(square) == rows(square)
        packed = column[b : b + 1, :] % blocks * width + far_ranks_ref[b : b + 1, :]
        packed = jnp.sum(jnp.where(side, packed, 0).astype(F32), axis=1, keepdims=True).astype(jnp.int32)
        kept = (lane // rank == packed // width) & (lane % rank < packed % width)
        keep_ref[b * far_count : (b + 1) * far_count, :] = kept.astype(F32)
        square = (near_count, near_count)
        side = lanes(square) == rows(square)
        picked = jnp.where(side, near_columns_ref[b : b + 1, :], 0).astype(F32)
        picked = jnp.sum(picked, axis=1, keepdims=True).astype(jnp.int32)
        near_pick_ref[b * near_count : (b + 1) * near_count, :] = (lanes((near_count, width)) == picked).astype(F32)
    for c in range(CORES):
        half = side_ref[c, 0:chips, :]
        half = jnp.where(core == 0, half, pltpu.roll(half, width - 2 * slots, 1))
        turn = FIRST_CHIP % chips
        tail_ref[pl.ds(c + CORES * turn, chips - turn, stride=CORES), :] = half[: chips - turn, :]
        tail_ref[pl.ds(c, turn, stride=CORES), :] = half[chips - turn :, :]
    tail = tail_ref[...]
    slot = rows((groups, width)) * slots
    for b in range(blocks):
        trace = jnp.zeros((groups, width), F32)
        for s in range(slots):
            trace = trace + jnp.where(source_ref[b : b + 1, :] - s == slot, tail[:, s : s + 1], 0.0)
        trace_ref[b : b + 1, :] = 0.5 * jnp.sum(trace, axis=0, keepdims=True)
    index = slot_columns(send_ref)
    bits = width.bit_length() - 1
    added = None
    for s in range(slots):
        column = jnp.broadcast_to(index[:, s : s + 1], (groups, width))
        choice = (lanes((groups, 2 * height)) == (column >> bits)[:, 0 : 2 * height]).astype(BF16)
        value = jnp.where(lanes((groups, width)) == (column & (width - 1)), tail[:, slots + s : slots + s + 1], 0.0)
        term = dot_exact(choice, value, ((0,), (0,)))
        added = term if added is None else added + term
    edge_x = edge_ref[0]
    edge_y = edge_ref[1]
    shape = (height, width)
    lane = lanes(shape)
    line = rows(shape)
    own = side_ref[1 - core, chips : chips + 1, :]
    other = side_ref[1 - core, chips + SIDE // 2 : chips + SIDE // 2 + 1, :]
    above = jnp.where(core == 0, other, own)
    below = jnp.where(core == 0, own, other)
    next_x = jnp.where(lane == width - 1, 0.0, pltpu.roll(edge_x, width - 1, 1))
    next_y = jnp.where(line == height - 1, below, pltpu.roll(edge_y, height - 1, 0))
    flux = next_y - edge_y - next_x + edge_x
    flux_left = jnp.where(lane == 0, -edge_x, pltpu.roll(flux, 1, 1))
    flux_up = jnp.where(line == 0, edge_y + above, pltpu.roll(flux, 1, 0))
    volume_ref[0] = flux_left - flux + conductance_ref[0] * edge_x + added[0:height, :]
    volume_ref[1] = flux_up - flux + conductance_ref[1] * edge_y + added[height : 2 * height, :]
    for copy in copies[-2:]:
        copy.wait()


def finish_kernel(
    members,
    chips,
    volume_in,
    trace_ref,
    index_ref,
    keep_ref,
    near_pick_ref,
    every_ref,
    near_ref,
    coupling_ref,
    left_ref,
    volume_ref,
    surface_ref,
    picked_ref,
    vector_ref,
):
    blocks, width = trace_ref.shape
    height = volume_ref.shape[1]
    rank = left_ref.shape[1]
    per_member = chips + blocks + 1
    per_core = members * per_member
    core = lax.rem(lax.axis_index("group"), CORES)
    member = lax.axis_index("member")
    near_count = near_ref.shape[1]
    far_count = coupling_ref.shape[1]
    here = side_of(member, members)
    fields = []
    for m in range(members):
        held = lax.rem(core + side_of(m, members) + here, CORES)
        row = held * per_core + spot(m, FIRST_MEMBER, members) * per_member + chips
        fields.append(every_ref[pl.ds(row, blocks), :])
    choice = near_pick_ref[:, 0 : members * blocks].astype(BF16)
    vector_ref[...] = dot_exact(choice, jnp.concatenate(fields, axis=0), ((1,), (0,)))
    sums = []
    for b in range(blocks):
        total = jnp.zeros((width, width), F32)
        for n in range(near_count):
            at = b * near_count + n
            total = total + near_ref[b, n] * vector_ref[at : at + 1, :]
        sums.append(total)
    near = dot_exact(jnp.ones((8, width), BF16), jnp.concatenate(sums, axis=0), ((1,), (1,)))
    for b in range(blocks):
        for f in range(far_count):
            at = b * far_count + f
            picked_ref[at : at + 1, :] = every_ref[pl.ds(index_ref[0, at], 1), :]
    picked = jnp.where(keep_ref[...] > 0.0, picked_ref[...], 0.0)
    folded = picked
    for q in range(1, width // rank):
        folded = folded + pltpu.roll(picked, q * rank, 1)
    picked_ref[...] = folded
    for b in range(blocks):
        total = jnp.zeros((rank, rank), F32)
        for f in range(far_count):
            at = b * far_count + f
            total = total + coupling_ref[b, f] * picked_ref[at : at + 1, 0:rank]
        summed = jnp.sum(total, axis=1, keepdims=True)
        far = jnp.sum(left_ref[b] * summed, axis=0, keepdims=True)
        surface_ref[b : b + 1, :] = near[0:1, b * width : (b + 1) * width] + far + trace_ref[b : b + 1, :]

    ends = chips + blocks

    def rim_of(other):
        inside = jnp.where((other >= 0) & (other < members), 1.0, 0.0)
        other = lax.clamp(0, other, members - 1)
        held = lax.rem(core + side_of(other, members) + here, CORES)
        row = spot(other, FIRST_MEMBER, members) * per_member + ends
        mine = every_ref[pl.ds(held * per_core + row, 1), :] * inside
        theirs = every_ref[pl.ds((1 - held) * per_core + row, 1), :] * inside
        return mine, theirs

    mine, theirs = rim_of(member - 1)
    mine_after, theirs_after = rim_of(member + 1)
    shape = (height, width)
    lane = lanes(shape)
    line = rows(shape)
    corner_y = 2 * height + jnp.where(core == 0, 0, 3 * height // 2)
    left = upright(mine, 0, shape)
    left = left + jnp.where(line[:, 0:1] == height - 1, upright(theirs, corner_y - height + 1, shape), 0.0)
    right = upright(mine_after, height, shape)
    corner_x = jnp.where(core == 0, 3 * height, 2 * height - 1)
    corner = jnp.sum(jnp.where(lanes((1, width)) == corner_x, theirs_after, 0.0), axis=1, keepdims=True)
    end = jnp.where(lane == width - 1, right, 0.0)
    volume_ref[0] = volume_in[0] + jnp.where(lane == 0, left, 0.0) + end
    last = jnp.where(lane == width - 1, 1.0, 0.0)
    up = jnp.where(line == 0, corner, pltpu.roll(jnp.broadcast_to(right, shape), 1, 0))
    volume_ref[1] = volume_in[1] + end - last * up


def vmem(count):
    return [pl.BlockSpec(memory_space=pltpu.VMEM)] * count


PARAMS = pltpu.CompilerParams(vmem_limit_bytes=16 * 1024 * 1024)


def body(
    edge_field,
    conductance,
    send_index,
    panel_source,
    surface_field,
    near_columns,
    near_tiles,
    far_columns,
    far_ranks,
    far_coupling,
    basis_left,
    basis_right,
):
    groups = lax.axis_size("group")
    members = lax.axis_size("member")
    slots = send_index.shape[2]
    blocks, width = surface_field.shape
    chips = groups // CORES
    per_member = chips + blocks + 1
    send = jnp.transpose(send_index, (2, 0, 1))
    right = jnp.swapaxes(basis_right, 1, 2)
    left = jnp.swapaxes(basis_left, 1, 2)
    near_count = near_columns.shape[1]
    far_count = far_columns.shape[1]
    chip_order = [(FIRST_CHIP + chip) % chips for chip in range(chips)]
    member_order = [(FIRST_MEMBER + member) % members for member in range(members)]
    one_core = [[chip * CORES + core for chip in chip_order] for core in range(CORES)]
    crossed = [
        [(chip * CORES + (core + side_of(m, members)) % CORES) * members + m for m in member_order]
        for chip in range(chips)
        for core in range(CORES)
    ]
    one_chip = [[chip * CORES + core for core in range(CORES)] for chip in range(chips)]

    hbm = pl.BlockSpec(memory_space=pltpu.HBM)
    edge_field, conductance, send, panel_source, surface_field, right, left, far_coupling = [
        pltpu.with_memory_space_constraint(array, pltpu.HBM)
        for array in (edge_field, conductance, send, panel_source, surface_field, right, left, far_coupling)
    ]
    near_columns, far_columns, far_ranks = [
        pltpu.with_memory_space_constraint(array, pltpu.HBM) for array in (near_columns, far_columns, far_ranks)
    ]

    def like(array):
        return pltpu.VMEM(array.shape, array.dtype)

    def out(*shape, dtype=F32):
        return jax.ShapeDtypeStruct(shape, dtype)

    first, rim = pl.pallas_call(
        pack_kernel,
        name="pack",
        out_shape=(out(chips * ROWS, width), out(blocks + 2, width)),
        in_specs=[hbm] * 5,
        out_specs=tuple(vmem(2)),
        scratch_shapes=[
            like(edge_field),
            like(send),
            like(panel_source),
            like(surface_field),
            like(right),
            pltpu.VMEM((groups, width), F32),
            pltpu.SemaphoreType.DMA((5,)),
        ],
        compiler_params=PARAMS,
    )(edge_field, send, panel_source, surface_field, right)
    first = lax.all_to_all(
        first.reshape(chips, 1, ROWS * width),
        "group",
        split_axis=0,
        concat_axis=0,
        axis_index_groups=one_core,
        tiled=True,
    ).reshape(chips * ROWS, width)
    second, side = pl.pallas_call(
        functools.partial(spread_kernel, members, slots),
        name="spread",
        out_shape=(out(members * per_member, width), out(chips + SIDE, width)),
        in_specs=vmem(2),
        out_specs=tuple(vmem(2)),
        scratch_shapes=[pltpu.VMEM((per_member, width), F32)],
        compiler_params=PARAMS,
    )(first, rim)
    second = lax.all_to_all(
        second.reshape(members, 1, per_member * width),
        ("group", "member"),
        split_axis=0,
        concat_axis=0,
        axis_index_groups=crossed,
        tiled=True,
    )
    side = lax.all_gather(side, "group", axis=0, axis_index_groups=one_chip, tiled=True)
    volume, trace, index, keep, near_pick, coupling, left = pl.pallas_call(
        functools.partial(local_kernel, members),
        name="local",
        out_shape=(
            out(*edge_field.shape),
            out(blocks, width),
            out(1, width, dtype=jnp.int32),
            out(blocks * far_count, width),
            out(blocks * near_count, width),
            out(*far_coupling.shape),
            out(*left.shape),
        ),
        in_specs=[hbm] * 9 + vmem(1),
        out_specs=tuple(vmem(7)),
        scratch_shapes=[
            like(edge_field),
            like(conductance),
            like(send),
            like(panel_source),
            like(near_columns),
            like(far_columns),
            like(far_ranks),
            pltpu.VMEM((groups, width), F32),
            pltpu.SemaphoreType.DMA((9,)),
        ],
        compiler_params=PARAMS,
        cost_estimate=pl.CostEstimate(flops=10_000_000, bytes_accessed=2_500_000, transcendentals=0),
    )(
        edge_field,
        conductance,
        send,
        panel_source,
        near_columns,
        far_columns,
        far_ranks,
        far_coupling,
        left,
        side.reshape(CORES, chips + SIDE, width),
    )
    every = lax.all_gather(
        second.reshape(members * per_member, width),
        "group",
        axis=0,
        axis_index_groups=one_chip,
        tiled=True,
    )
    return pl.pallas_call(
        functools.partial(finish_kernel, members, chips),
        name="finish",
        out_shape=(out(*edge_field.shape), out(blocks, width)),
        in_specs=vmem(9),
        out_specs=tuple(vmem(2)),
        scratch_shapes=[
            pltpu.VMEM((blocks * far_count, width), F32),
            pltpu.VMEM((blocks * near_count, width), F32),
        ],
        compiler_params=PARAMS,
    )(volume, trace, index, keep, near_pick, every, near_tiles, coupling, left)


def solution(mesh):
    both = ("group", "member")
    placed = (
        P(None, "group", "member"),
        P(None, "group", "member"),
        P(both, None, None),
        P(both, None),
        P(both, None),
        P(both, None),
        P(both, None, None, None),
        P(both, None),
        P(both, None),
        P(both, None, None, None),
        P(both, None, None),
        P(both, None, None),
    )
    return jax.shard_map(
        body,
        mesh=mesh,
        in_specs=placed,
        out_specs=(P(None, "group", "member"), P(both, None)),
        check_vma=False,
    )
```

```python
import functools

import jax
import jax.numpy as jnp
from jax import lax
from jax.experimental import pallas as pl
from jax.experimental.pallas import tpu as pltpu
from jax.sharding import PartitionSpec as P

F32 = jnp.float32
BF16 = jnp.bfloat16
HIGHEST = lax.Precision.HIGHEST
FIRST_CHIP = 34
FIRST_MEMBER = 4
CORES = 2
ROWS = 3
SIDE = 8


def split3(value):
    first = value.astype(BF16)
    rest = value - first.astype(F32)
    second = rest.astype(BF16)
    third = (rest - second.astype(F32)).astype(BF16)
    return first, second, third


def dot_exact(choice, value, dims):
    total = None
    for part in split3(value):
        term = lax.dot_general(choice, part, (dims, ((), ())), preferred_element_type=F32)
        total = term if total is None else total + term
    return total


def dot_full(left, right, dims):
    return lax.dot_general(left, right, (dims, ((), ())), precision=HIGHEST, preferred_element_type=F32)


def lanes(shape):
    return lax.broadcasted_iota(jnp.int32, shape, len(shape) - 1)


def rows(shape):
    return lax.broadcasted_iota(jnp.int32, shape, len(shape) - 2)


def upright(row, start, shape):
    wide = jnp.where(lanes(shape) == rows(shape) + start, row, 0.0)
    return jnp.sum(wide, axis=1, keepdims=True)


def spot(index, first, count):
    return (index + (count - first % count)) % count


def side_of(member, members):
    return 2 * member // members


def fetch(pairs, sems):
    copies = [pltpu.make_async_copy(source, target, sems.at[i]) for i, (source, target) in enumerate(pairs)]
    for copy in copies:
        copy.start()
    return copies


def slot_columns(send_ref):
    slots, _, groups = send_ref.shape
    rest = jnp.zeros((8 - slots, groups), jnp.int32)
    return jnp.concatenate([send_ref[s] for s in range(slots)] + [rest], axis=0).T


def pack_kernel(
    edge_in,
    send_in,
    source_in,
    surface_in,
    right_in,
    out_ref,
    rim_ref,
    edge_ref,
    send_ref,
    source_ref,
    surface_ref,
    right_ref,
    tail_ref,
    sems,
):
    blocks, width = surface_ref.shape
    rank = right_ref.shape[1]
    height = edge_ref.shape[1]
    slots, _, groups = send_ref.shape
    chips = groups // CORES
    bits = width.bit_length() - 1
    copies = fetch(
        (
            (edge_in, edge_ref),
            (send_in, send_ref),
            (surface_in, surface_ref),
            (source_in, source_ref),
            (right_in, right_ref),
        ),
        sems,
    )
    core = lax.rem(lax.axis_index("group"), CORES)
    for copy in copies[:2]:
        copy.wait()
    for copy in copies[2:]:
        copy.wait()
    edge_x = edge_ref[0]
    edge_y = edge_ref[1]
    last_x = edge_x[height - 1 : height, :]
    beyond = jnp.where(lanes((1, width)) == width - 1, 0.0, pltpu.roll(last_x, width - 1, 1))
    down = last_x - beyond - edge_y[height - 1 : height, :]
    rim = jnp.where(core == CORES - 1, down, edge_y[0:1, :])
    own = jnp.where(core == 0, down, edge_y[0:1, :])
    next_y = jnp.where(rows((height, width)) == height - 1, 0.0, pltpu.roll(edge_y, height - 1, 0))
    flow = next_y - edge_y + edge_x
    last = (lanes((8, width)) == width - 1).astype(BF16)
    first = (lanes((8, width)) == 0).astype(BF16)
    ends = jnp.concatenate(
        [
            dot_exact(last, flow, ((1,), (1,)))[0:1, :],
            dot_exact(first, edge_x, ((1,), (1,)))[0:1, :],
            jnp.broadcast_to(edge_y[0:1, width - 1 : width], (1, width - 2 * height)),
        ],
        axis=1,
    )
    parts = split3(edge_ref[...].reshape(2 * height, width))
    tall = (2 * height, groups)
    values = []
    for s in range(slots):
        index = send_ref[s]
        choice = (rows(tall) == (index >> bits)).astype(BF16)
        picked = None
        for part in parts:
            term = lax.dot_general(part, choice, (((0,), (0,)), ((), ())), preferred_element_type=F32)
            picked = term if picked is None else picked + term
        here = rows((width, groups)) == (index & (width - 1))
        values.append(jnp.sum(jnp.where(here, picked, 0.0), axis=0, keepdims=True))
    values = jnp.concatenate(values + [jnp.zeros((8 - slots, groups), F32)], axis=0).T
    lane = lanes((groups, width))
    tail = jnp.concatenate([values, jnp.zeros((groups, width - 8), F32)], axis=1)
    tail = jnp.where(lane == 2 * CORES * slots, last_x[0:1, 0:1], tail)
    slot = rows((groups, width)) * slots
    for s in range(slots):
        total = jnp.zeros((groups, width), F32)
        for b in range(blocks):
            total = total + jnp.where(source_ref[b : b + 1, :] - s == slot, surface_ref[b : b + 1, :], 0.0)
        tail = jnp.where(lane == slots + s, jnp.sum(total, axis=1, keepdims=True), tail)
    every = dot_full(surface_ref[...], right_ref[...].reshape(blocks * rank, width), ((1,), (1,)))
    mine = lanes((blocks, blocks * rank)) // rank == rows((blocks, blocks * rank))
    coeff = jnp.sum(jnp.where(mine, every, 0.0), axis=0, keepdims=True)
    out_ref[pl.ds(0, chips, stride=ROWS), :] = jnp.broadcast_to(coeff, (chips, width))
    out_ref[pl.ds(1, chips, stride=ROWS), :] = jnp.broadcast_to(rim, (chips, width))
    tail_ref[...] = tail
    lane = lanes((chips, width))
    even = tail_ref[pl.ds(0, chips, stride=CORES), :]
    odd = tail_ref[pl.ds(1, chips, stride=CORES), :]
    moved = pltpu.roll(odd, 2 * slots, 1)
    theirs = (lane >= 2 * slots) & (lane < 2 * CORES * slots)
    both = jnp.where(theirs, moved, even)
    turn = FIRST_CHIP % chips
    out_ref[pl.ds(2, chips - turn, stride=ROWS), :] = both[turn:, :]
    out_ref[pl.ds(2 + ROWS * (chips - turn), turn, stride=ROWS), :] = both[:turn, :]
    rim_ref[0:blocks, :] = surface_ref[...]
    rim_ref[blocks : blocks + 1, :] = ends
    rim_ref[blocks + 1 : blocks + 2, :] = own


def spread_kernel(members, slots, first_ref, rim_ref, out_ref, side_ref, block_ref):
    width = rim_ref.shape[1]
    chips = first_ref.shape[0] // ROWS
    blocks = rim_ref.shape[0] - 2
    per_member = chips + blocks + 1
    group = lax.axis_index("group")
    core = lax.rem(group, CORES)
    chip = group // CORES
    before = jnp.where(chip > 0, 1.0, 0.0)
    after = jnp.where(chip + 1 < chips, 1.0, 0.0)
    chip_before = spot(lax.max(chip - 1, 0), FIRST_CHIP, chips) * ROWS
    chip_after = spot(lax.min(chip + 1, chips - 1), FIRST_CHIP, chips) * ROWS
    rim_before = first_ref[pl.ds(chip_before + 1, 1), :] * before
    rim_after = first_ref[pl.ds(chip_after + 1, 1), :] * after
    corner_before = first_ref[pl.ds(chip_before + 2, 1), :] * before
    corners = 2 * CORES * slots
    lane = lanes((1, width))
    ends = rim_ref[blocks : blocks + 1, :]
    ends = jnp.where(lane >= 3 * width // 4, corner_before[:, corners : corners + 1], ends)
    ends = jnp.where(lane >= 7 * width // 8, rim_after[:, width - 1 : width], ends)
    block_ref[0:chips, :] = first_ref[pl.ds(0, chips, stride=ROWS), :]
    block_ref[chips : chips + blocks, :] = rim_ref[0:blocks, :]
    block_ref[chips + blocks : chips + blocks + 1, :] = ends
    for m in range(members):
        out_ref[m * per_member : (m + 1) * per_member, :] = block_ref[...]
    other = jnp.where(core == 0, rim_after, rim_before)
    side_ref[0:chips, :] = first_ref[pl.ds(2, chips, stride=ROWS), :]
    half = rows((SIDE, width)) < SIDE // 2
    side_ref[chips : chips + SIDE, :] = jnp.where(half, rim_ref[blocks + 1 : blocks + 2, :], other)


def local_kernel(
    members,
    edge_in,
    conductance_in,
    send_in,
    source_in,
    near_columns_in,
    far_columns_in,
    far_ranks_in,
    coupling_in,
    left_in,
    side_ref,
    volume_ref,
    trace_ref,
    index_ref,
    keep_ref,
    near_pick_ref,
    coupling_ref,
    left_ref,
    edge_ref,
    conductance_ref,
    send_ref,
    source_ref,
    near_columns_ref,
    far_columns_ref,
    far_ranks_ref,
    tail_ref,
    sems,
):
    copies = fetch(
        (
            (edge_in, edge_ref),
            (conductance_in, conductance_ref),
            (send_in, send_ref),
            (source_in, source_ref),
            (near_columns_in, near_columns_ref),
            (far_columns_in, far_columns_ref),
            (far_ranks_in, far_ranks_ref),
            (left_in, left_ref),
            (coupling_in, coupling_ref),
        ),
        sems,
    )
    for copy in copies[:-2]:
        copy.wait()
    blocks, width = source_ref.shape
    height = edge_ref.shape[1]
    slots, _, groups = send_ref.shape
    chips = groups // CORES
    rank = left_ref.shape[1]
    core = lax.rem(lax.axis_index("group"), CORES)
    near_count = near_columns_ref.shape[1]
    far_count = far_columns_ref.shape[1]
    column = far_columns_ref[...]
    device = column // blocks
    group = device // members
    per_member = chips + blocks + 1
    owner = device % members
    here = side_of(lax.axis_index("member"), members)
    held = (group + side_of(owner, members) + here) % CORES
    owner = spot(owner, FIRST_MEMBER, members)
    place = held * (members * per_member) + owner * per_member + spot(group // CORES, FIRST_CHIP, chips)
    rest = jnp.zeros((1, width - blocks * far_count), jnp.int32)
    index_ref[...] = jnp.concatenate([place[b : b + 1, :] for b in range(blocks)] + [rest], axis=1)
    lane = lanes((far_count, width))
    for b in range(blocks):
        square = (far_count, far_count)
        side = lanes(square) == rows(square)
        packed = column[b : b + 1, :] % blocks * width + far_ranks_ref[b : b + 1, :]
        packed = jnp.sum(jnp.where(side, packed, 0).astype(F32), axis=1, keepdims=True).astype(jnp.int32)
        kept = (lane // rank == packed // width) & (lane % rank < packed % width)
        keep_ref[b * far_count : (b + 1) * far_count, :] = kept.astype(F32)
        square = (near_count, near_count)
        side = lanes(square) == rows(square)
        picked = jnp.where(side, near_columns_ref[b : b + 1, :], 0).astype(F32)
        picked = jnp.sum(picked, axis=1, keepdims=True).astype(jnp.int32)
        near_pick_ref[b * near_count : (b + 1) * near_count, :] = (lanes((near_count, width)) == picked).astype(F32)
    for c in range(CORES):
        half = side_ref[c, 0:chips, :]
        half = jnp.where(core == 0, half, pltpu.roll(half, width - 2 * slots, 1))
        turn = FIRST_CHIP % chips
        tail_ref[pl.ds(c + CORES * turn, chips - turn, stride=CORES), :] = half[: chips - turn, :]
        tail_ref[pl.ds(c, turn, stride=CORES), :] = half[chips - turn :, :]
    tail = tail_ref[...]
    slot = rows((groups, width)) * slots
    for b in range(blocks):
        trace = jnp.zeros((groups, width), F32)
        for s in range(slots):
            trace = trace + jnp.where(source_ref[b : b + 1, :] - s == slot, tail[:, s : s + 1], 0.0)
        trace_ref[b : b + 1, :] = 0.5 * jnp.sum(trace, axis=0, keepdims=True)
    index = slot_columns(send_ref)
    bits = width.bit_length() - 1
    added = None
    for s in range(slots):
        column = jnp.broadcast_to(index[:, s : s + 1], (groups, width))
        choice = (lanes((groups, 2 * height)) == (column >> bits)[:, 0 : 2 * height]).astype(BF16)
        value = jnp.where(lanes((groups, width)) == (column & (width - 1)), tail[:, slots + s : slots + s + 1], 0.0)
        term = dot_exact(choice, value, ((0,), (0,)))
        added = term if added is None else added + term
    edge_x = edge_ref[0]
    edge_y = edge_ref[1]
    shape = (height, width)
    lane = lanes(shape)
    line = rows(shape)
    own = side_ref[1 - core, chips : chips + 1, :]
    other = side_ref[1 - core, chips + SIDE // 2 : chips + SIDE // 2 + 1, :]
    above = jnp.where(core == 0, other, own)
    below = jnp.where(core == 0, own, other)
    next_x = jnp.where(lane == width - 1, 0.0, pltpu.roll(edge_x, width - 1, 1))
    next_y = jnp.where(line == height - 1, below, pltpu.roll(edge_y, height - 1, 0))
    flux = next_y - edge_y - next_x + edge_x
    flux_left = jnp.where(lane == 0, -edge_x, pltpu.roll(flux, 1, 1))
    flux_up = jnp.where(line == 0, edge_y + above, pltpu.roll(flux, 1, 0))
    volume_ref[0] = flux_left - flux + conductance_ref[0] * edge_x + added[0:height, :]
    volume_ref[1] = flux_up - flux + conductance_ref[1] * edge_y + added[height : 2 * height, :]
    for copy in copies[-2:]:
        copy.wait()


def finish_kernel(
    members,
    chips,
    volume_in,
    trace_ref,
    index_ref,
    keep_ref,
    near_pick_ref,
    every_ref,
    near_ref,
    coupling_ref,
    left_ref,
    volume_ref,
    surface_ref,
    picked_ref,
    vector_ref,
):
    blocks, width = trace_ref.shape
    height = volume_ref.shape[1]
    rank = left_ref.shape[1]
    per_member = chips + blocks + 1
    per_core = members * per_member
    core = lax.rem(lax.axis_index("group"), CORES)
    member = lax.axis_index("member")
    near_count = near_ref.shape[1]
    far_count = coupling_ref.shape[1]
    here = side_of(member, members)
    fields = []
    for m in range(members):
        held = lax.rem(core + side_of(m, members) + here, CORES)
        row = held * per_core + spot(m, FIRST_MEMBER, members) * per_member + chips
        fields.append(every_ref[pl.ds(row, blocks), :])
    choice = near_pick_ref[:, 0 : members * blocks].astype(BF16)
    vector_ref[...] = dot_exact(choice, jnp.concatenate(fields, axis=0), ((1,), (0,)))
    sums = []
    for b in range(blocks):
        total = jnp.zeros((width, width), F32)
        for n in range(near_count):
            at = b * near_count + n
            total = total + near_ref[b, n] * vector_ref[at : at + 1, :]
        sums.append(total)
    near = dot_exact(jnp.ones((8, width), BF16), jnp.concatenate(sums, axis=0), ((1,), (1,)))
    for b in range(blocks):
        for f in range(far_count):
            at = b * far_count + f
            picked_ref[at : at + 1, :] = every_ref[pl.ds(index_ref[0, at], 1), :]
    picked = jnp.where(keep_ref[...] > 0.0, picked_ref[...], 0.0)
    folded = picked
    for q in range(1, width // rank):
        folded = folded + pltpu.roll(picked, q * rank, 1)
    picked_ref[...] = folded
    for b in range(blocks):
        total = jnp.zeros((rank, rank), F32)
        for f in range(far_count):
            at = b * far_count + f
            total = total + coupling_ref[b, f] * picked_ref[at : at + 1, 0:rank]
        summed = jnp.sum(total, axis=1, keepdims=True)
        far = jnp.sum(left_ref[b] * summed, axis=0, keepdims=True)
        surface_ref[b : b + 1, :] = near[0:1, b * width : (b + 1) * width] + far + trace_ref[b : b + 1, :]

    ends = chips + blocks

    def rim_of(other):
        inside = jnp.where((other >= 0) & (other < members), 1.0, 0.0)
        other = lax.clamp(0, other, members - 1)
        held = lax.rem(core + side_of(other, members) + here, CORES)
        row = spot(other, FIRST_MEMBER, members) * per_member + ends
        mine = every_ref[pl.ds(held * per_core + row, 1), :] * inside
        theirs = every_ref[pl.ds((1 - held) * per_core + row, 1), :] * inside
        return mine, theirs

    mine, theirs = rim_of(member - 1)
    mine_after, theirs_after = rim_of(member + 1)
    shape = (height, width)
    lane = lanes(shape)
    line = rows(shape)
    corner_y = 2 * height + jnp.where(core == 0, 0, 3 * height // 2)
    left = upright(mine, 0, shape)
    left = left + jnp.where(line[:, 0:1] == height - 1, upright(theirs, corner_y - height + 1, shape), 0.0)
    right = upright(mine_after, height, shape)
    corner_x = jnp.where(core == 0, 3 * height, 2 * height - 1)
    corner = jnp.sum(jnp.where(lanes((1, width)) == corner_x, theirs_after, 0.0), axis=1, keepdims=True)
    end = jnp.where(lane == width - 1, right, 0.0)
    volume_ref[0] = volume_in[0] + jnp.where(lane == 0, left, 0.0) + end
    last = jnp.where(lane == width - 1, 1.0, 0.0)
    up = jnp.where(line == 0, corner, pltpu.roll(jnp.broadcast_to(right, shape), 1, 0))
    volume_ref[1] = volume_in[1] + end - last * up


def vmem(count):
    return [pl.BlockSpec(memory_space=pltpu.VMEM)] * count


PARAMS = pltpu.CompilerParams(vmem_limit_bytes=16 * 1024 * 1024)


def body(
    edge_field,
    conductance,
    send_index,
    panel_source,
    surface_field,
    near_columns,
    near_tiles,
    far_columns,
    far_ranks,
    far_coupling,
    basis_left,
    basis_right,
):
    groups = lax.axis_size("group")
    members = lax.axis_size("member")
    slots = send_index.shape[2]
    blocks, width = surface_field.shape
    chips = groups // CORES
    per_member = chips + blocks + 1
    send = jnp.transpose(send_index, (2, 0, 1))
    right = jnp.swapaxes(basis_right, 1, 2)
    left = jnp.swapaxes(basis_left, 1, 2)
    near_count = near_columns.shape[1]
    far_count = far_columns.shape[1]
    chip_order = [(FIRST_CHIP + chip) % chips for chip in range(chips)]
    member_order = [(FIRST_MEMBER + member) % members for member in range(members)]
    one_core = [[chip * CORES + core for chip in chip_order] for core in range(CORES)]
    crossed = [
        [(chip * CORES + (core + side_of(m, members)) % CORES) * members + m for m in member_order]
        for chip in range(chips)
        for core in range(CORES)
    ]
    one_chip = [[chip * CORES + core for core in range(CORES)] for chip in range(chips)]

    hbm = pl.BlockSpec(memory_space=pltpu.HBM)
    edge_field, conductance, send, panel_source, surface_field, right, left, far_coupling = [
        pltpu.with_memory_space_constraint(array, pltpu.HBM)
        for array in (edge_field, conductance, send, panel_source, surface_field, right, left, far_coupling)
    ]
    near_columns, far_columns, far_ranks = [
        pltpu.with_memory_space_constraint(array, pltpu.HBM) for array in (near_columns, far_columns, far_ranks)
    ]

    def like(array):
        return pltpu.VMEM(array.shape, array.dtype)

    def out(*shape, dtype=F32):
        return jax.ShapeDtypeStruct(shape, dtype)

    first, rim = pl.pallas_call(
        pack_kernel,
        name="pack",
        out_shape=(out(chips * ROWS, width), out(blocks + 2, width)),
        in_specs=[hbm] * 5,
        out_specs=tuple(vmem(2)),
        scratch_shapes=[
            like(edge_field),
            like(send),
            like(panel_source),
            like(surface_field),
            like(right),
            pltpu.VMEM((groups, width), F32),
            pltpu.SemaphoreType.DMA((5,)),
        ],
        compiler_params=PARAMS,
    )(edge_field, send, panel_source, surface_field, right)
    first = lax.all_to_all(
        first.reshape(chips, 1, ROWS * width),
        "group",
        split_axis=0,
        concat_axis=0,
        axis_index_groups=one_core,
        tiled=True,
    ).reshape(chips * ROWS, width)
    second, side = pl.pallas_call(
        functools.partial(spread_kernel, members, slots),
        name="spread",
        out_shape=(out(members * per_member, width), out(chips + SIDE, width)),
        in_specs=vmem(2),
        out_specs=tuple(vmem(2)),
        scratch_shapes=[pltpu.VMEM((per_member, width), F32)],
        compiler_params=PARAMS,
    )(first, rim)
    second = lax.all_to_all(
        second.reshape(members, 1, per_member * width),
        ("group", "member"),
        split_axis=0,
        concat_axis=0,
        axis_index_groups=crossed,
        tiled=True,
    )
    side = lax.all_gather(side, "group", axis=0, axis_index_groups=one_chip, tiled=True)
    volume, trace, index, keep, near_pick, coupling, left = pl.pallas_call(
        functools.partial(local_kernel, members),
        name="local",
        out_shape=(
            out(*edge_field.shape),
            out(blocks, width),
            out(1, width, dtype=jnp.int32),
            out(blocks * far_count, width),
            out(blocks * near_count, width),
            out(*far_coupling.shape),
            out(*left.shape),
        ),
        in_specs=[hbm] * 9 + vmem(1),
        out_specs=tuple(vmem(7)),
        scratch_shapes=[
            like(edge_field),
            like(conductance),
            like(send),
            like(panel_source),
            like(near_columns),
            like(far_columns),
            like(far_ranks),
            pltpu.VMEM((groups, width), F32),
            pltpu.SemaphoreType.DMA((9,)),
        ],
        compiler_params=PARAMS,
        cost_estimate=pl.CostEstimate(flops=10_000_000, bytes_accessed=2_500_000, transcendentals=0),
    )(
        edge_field,
        conductance,
        send,
        panel_source,
        near_columns,
        far_columns,
        far_ranks,
        far_coupling,
        left,
        side.reshape(CORES, chips + SIDE, width),
    )
    every = lax.all_gather(
        second.reshape(members * per_member, width),
        "group",
        axis=0,
        axis_index_groups=one_chip,
        tiled=True,
    )
    return pl.pallas_call(
        functools.partial(finish_kernel, members, chips),
        name="finish",
        out_shape=(out(*edge_field.shape), out(blocks, width)),
        in_specs=vmem(9),
        out_specs=tuple(vmem(2)),
        scratch_shapes=[
            pltpu.VMEM((blocks * far_count, width), F32),
            pltpu.VMEM((blocks * near_count, width), F32),
        ],
        compiler_params=PARAMS,
    )(volume, trace, index, keep, near_pick, every, near_tiles, coupling, left)


def solution(mesh):
    both = ("group", "member")
    placed = (
        P(None, "group", "member"),
        P(None, "group", "member"),
        P(both, None, None),
        P(both, None),
        P(both, None),
        P(both, None),
        P(both, None, None, None),
        P(both, None),
        P(both, None),
        P(both, None, None, None),
        P(both, None, None),
        P(both, None, None),
    )
    return jax.shard_map(
        body,
        mesh=mesh,
        in_specs=placed,
        out_specs=(P(None, "group", "member"), P(both, None)),
        check_vma=False,
    )
```

```python
import functools

import jax
import jax.numpy as jnp
from jax import lax
from jax.experimental import pallas as pl
from jax.experimental.pallas import tpu as pltpu
from jax.sharding import PartitionSpec as P

F32 = jnp.float32
BF16 = jnp.bfloat16
HIGHEST = lax.Precision.HIGHEST
FIRST_CHIP = 38
FIRST_MEMBER = 4
CORES = 2
ROWS = 3
SIDE = 8


def split3(value):
    first = value.astype(BF16)
    rest = value - first.astype(F32)
    second = rest.astype(BF16)
    third = (rest - second.astype(F32)).astype(BF16)
    return first, second, third


def dot_exact(choice, value, dims):
    total = None
    for part in split3(value):
        term = lax.dot_general(choice, part, (dims, ((), ())), preferred_element_type=F32)
        total = term if total is None else total + term
    return total


def dot_full(left, right, dims):
    return lax.dot_general(left, right, (dims, ((), ())), precision=HIGHEST, preferred_element_type=F32)


def lanes(shape):
    return lax.broadcasted_iota(jnp.int32, shape, len(shape) - 1)


def rows(shape):
    return lax.broadcasted_iota(jnp.int32, shape, len(shape) - 2)


def upright(row, start, shape):
    wide = jnp.where(lanes(shape) == rows(shape) + start, row, 0.0)
    return jnp.sum(wide, axis=1, keepdims=True)


def spot(index, first, count):
    return (index + (count - first % count)) % count


def side_of(member, members):
    return 2 * member // members


def fetch(pairs, sems):
    copies = [pltpu.make_async_copy(source, target, sems.at[i]) for i, (source, target) in enumerate(pairs)]
    for copy in copies:
        copy.start()
    return copies


def slot_columns(send_ref):
    slots, _, groups = send_ref.shape
    rest = jnp.zeros((8 - slots, groups), jnp.int32)
    return jnp.concatenate([send_ref[s] for s in range(slots)] + [rest], axis=0).T


def pack_kernel(
    edge_in,
    send_in,
    source_in,
    surface_in,
    right_in,
    out_ref,
    rim_ref,
    edge_ref,
    send_ref,
    source_ref,
    surface_ref,
    right_ref,
    tail_ref,
    sems,
):
    blocks, width = surface_ref.shape
    rank = right_ref.shape[1]
    height = edge_ref.shape[1]
    slots, _, groups = send_ref.shape
    chips = groups // CORES
    bits = width.bit_length() - 1
    copies = fetch(
        (
            (edge_in, edge_ref),
            (send_in, send_ref),
            (surface_in, surface_ref),
            (source_in, source_ref),
            (right_in, right_ref),
        ),
        sems,
    )
    core = lax.rem(lax.axis_index("group"), CORES)
    for copy in copies[:2]:
        copy.wait()
    for copy in copies[2:]:
        copy.wait()
    edge_x = edge_ref[0]
    edge_y = edge_ref[1]
    last_x = edge_x[height - 1 : height, :]
    beyond = jnp.where(lanes((1, width)) == width - 1, 0.0, pltpu.roll(last_x, width - 1, 1))
    down = last_x - beyond - edge_y[height - 1 : height, :]
    rim = jnp.where(core == CORES - 1, down, edge_y[0:1, :])
    own = jnp.where(core == 0, down, edge_y[0:1, :])
    next_y = jnp.where(rows((height, width)) == height - 1, 0.0, pltpu.roll(edge_y, height - 1, 0))
    flow = next_y - edge_y + edge_x
    last = (lanes((8, width)) == width - 1).astype(BF16)
    first = (lanes((8, width)) == 0).astype(BF16)
    ends = jnp.concatenate(
        [
            dot_exact(last, flow, ((1,), (1,)))[0:1, :],
            dot_exact(first, edge_x, ((1,), (1,)))[0:1, :],
            jnp.broadcast_to(edge_y[0:1, width - 1 : width], (1, width - 2 * height)),
        ],
        axis=1,
    )
    index = slot_columns(send_ref)
    parts = split3(edge_ref[...].reshape(2 * height, width))
    lane = lanes((groups, width))
    tail = jnp.where(lane == 2 * CORES * slots, last_x[0:1, 0:1], 0.0)
    for s in range(slots):
        column = jnp.broadcast_to(index[:, s : s + 1], (groups, width))
        choice = (lanes((groups, 2 * height)) == (column >> bits)[:, 0 : 2 * height]).astype(BF16)
        picked = None
        for part in parts:
            term = lax.dot_general(choice, part, (((1,), (0,)), ((), ())), preferred_element_type=F32)
            picked = term if picked is None else picked + term
        value = jnp.sum(jnp.where(lane == (column & (width - 1)), picked, 0.0), axis=1, keepdims=True)
        tail = jnp.where(lane == s, value, tail)
    slot = rows((groups, width)) * slots
    for s in range(slots):
        total = jnp.zeros((groups, width), F32)
        for b in range(blocks):
            total = total + jnp.where(source_ref[b : b + 1, :] - s == slot, surface_ref[b : b + 1, :], 0.0)
        tail = jnp.where(lane == slots + s, jnp.sum(total, axis=1, keepdims=True), tail)
    every = dot_full(surface_ref[...], right_ref[...].reshape(blocks * rank, width), ((1,), (1,)))
    mine = lanes((blocks, blocks * rank)) // rank == rows((blocks, blocks * rank))
    coeff = jnp.sum(jnp.where(mine, every, 0.0), axis=0, keepdims=True)
    out_ref[pl.ds(0, chips, stride=ROWS), :] = jnp.broadcast_to(coeff, (chips, width))
    out_ref[pl.ds(1, chips, stride=ROWS), :] = jnp.broadcast_to(rim, (chips, width))
    tail_ref[...] = tail
    lane = lanes((chips, width))
    even = tail_ref[pl.ds(0, chips, stride=CORES), :]
    odd = tail_ref[pl.ds(1, chips, stride=CORES), :]
    moved = pltpu.roll(odd, 2 * slots, 1)
    theirs = (lane >= 2 * slots) & (lane < 2 * CORES * slots)
    both = jnp.where(theirs, moved, even)
    turn = FIRST_CHIP % chips
    out_ref[pl.ds(2, chips - turn, stride=ROWS), :] = both[turn:, :]
    out_ref[pl.ds(2 + ROWS * (chips - turn), turn, stride=ROWS), :] = both[:turn, :]
    rim_ref[0:blocks, :] = surface_ref[...]
    rim_ref[blocks : blocks + 1, :] = ends
    rim_ref[blocks + 1 : blocks + 2, :] = own


def spread_kernel(members, slots, first_ref, rim_ref, out_ref, side_ref, block_ref):
    width = rim_ref.shape[1]
    chips = first_ref.shape[0] // ROWS
    blocks = rim_ref.shape[0] - 2
    per_member = chips + blocks + 1
    group = lax.axis_index("group")
    core = lax.rem(group, CORES)
    chip = group // CORES
    before = jnp.where(chip > 0, 1.0, 0.0)
    after = jnp.where(chip + 1 < chips, 1.0, 0.0)
    chip_before = spot(lax.max(chip - 1, 0), FIRST_CHIP, chips) * ROWS
    chip_after = spot(lax.min(chip + 1, chips - 1), FIRST_CHIP, chips) * ROWS
    rim_before = first_ref[pl.ds(chip_before + 1, 1), :] * before
    rim_after = first_ref[pl.ds(chip_after + 1, 1), :] * after
    corner_before = first_ref[pl.ds(chip_before + 2, 1), :] * before
    corners = 2 * CORES * slots
    lane = lanes((1, width))
    ends = rim_ref[blocks : blocks + 1, :]
    ends = jnp.where(lane >= 3 * width // 4, corner_before[:, corners : corners + 1], ends)
    ends = jnp.where(lane >= 7 * width // 8, rim_after[:, width - 1 : width], ends)
    block_ref[0:chips, :] = first_ref[pl.ds(0, chips, stride=ROWS), :]
    block_ref[chips : chips + blocks, :] = rim_ref[0:blocks, :]
    block_ref[chips + blocks : chips + blocks + 1, :] = ends
    for m in range(members):
        out_ref[m * per_member : (m + 1) * per_member, :] = block_ref[...]
    other = jnp.where(core == 0, rim_after, rim_before)
    side_ref[0:chips, :] = first_ref[pl.ds(2, chips, stride=ROWS), :]
    half = rows((SIDE, width)) < SIDE // 2
    side_ref[chips : chips + SIDE, :] = jnp.where(half, rim_ref[blocks + 1 : blocks + 2, :], other)


def local_kernel(
    members,
    edge_in,
    conductance_in,
    send_in,
    source_in,
    near_columns_in,
    far_columns_in,
    far_ranks_in,
    coupling_in,
    left_in,
    side_ref,
    volume_ref,
    trace_ref,
    index_ref,
    keep_ref,
    near_pick_ref,
    coupling_ref,
    left_ref,
    edge_ref,
    conductance_ref,
    send_ref,
    source_ref,
    near_columns_ref,
    far_columns_ref,
    far_ranks_ref,
    tail_ref,
    sems,
):
    copies = fetch(
        (
            (edge_in, edge_ref),
            (conductance_in, conductance_ref),
            (send_in, send_ref),
            (source_in, source_ref),
            (near_columns_in, near_columns_ref),
            (far_columns_in, far_columns_ref),
            (far_ranks_in, far_ranks_ref),
            (left_in, left_ref),
            (coupling_in, coupling_ref),
        ),
        sems,
    )
    for copy in copies[:-2]:
        copy.wait()
    blocks, width = source_ref.shape
    height = edge_ref.shape[1]
    slots, _, groups = send_ref.shape
    chips = groups // CORES
    rank = left_ref.shape[1]
    core = lax.rem(lax.axis_index("group"), CORES)
    near_count = near_columns_ref.shape[1]
    far_count = far_columns_ref.shape[1]
    column = far_columns_ref[...]
    device = column // blocks
    group = device // members
    per_member = chips + blocks + 1
    owner = device % members
    here = side_of(lax.axis_index("member"), members)
    held = (group + side_of(owner, members) + here + 1) % CORES
    owner = spot(owner, FIRST_MEMBER, members)
    place = held * (members * per_member) + owner * per_member + spot(group // CORES, FIRST_CHIP, chips)
    rest = jnp.zeros((1, width - blocks * far_count), jnp.int32)
    index_ref[...] = jnp.concatenate([place[b : b + 1, :] for b in range(blocks)] + [rest], axis=1)
    lane = lanes((far_count, width))
    for b in range(blocks):
        square = (far_count, far_count)
        side = lanes(square) == rows(square)
        packed = column[b : b + 1, :] % blocks * width + far_ranks_ref[b : b + 1, :]
        packed = jnp.sum(jnp.where(side, packed, 0).astype(F32), axis=1, keepdims=True).astype(jnp.int32)
        kept = (lane // rank == packed // width) & (lane % rank < packed % width)
        keep_ref[b * far_count : (b + 1) * far_count, :] = kept.astype(F32)
        square = (near_count, near_count)
        side = lanes(square) == rows(square)
        picked = jnp.where(side, near_columns_ref[b : b + 1, :], 0).astype(F32)
        picked = jnp.sum(picked, axis=1, keepdims=True).astype(jnp.int32)
        near_pick_ref[b * near_count : (b + 1) * near_count, :] = (lanes((near_count, width)) == picked).astype(F32)
    for c in range(CORES):
        half = side_ref[CORES - 1 - c, 0:chips, :]
        half = jnp.where(core == 0, half, pltpu.roll(half, width - 2 * slots, 1))
        turn = FIRST_CHIP % chips
        tail_ref[pl.ds(c + CORES * turn, chips - turn, stride=CORES), :] = half[: chips - turn, :]
        tail_ref[pl.ds(c, turn, stride=CORES), :] = half[chips - turn :, :]
    tail = tail_ref[...]
    slot = rows((groups, width)) * slots
    for b in range(blocks):
        trace = jnp.zeros((groups, width), F32)
        for s in range(slots):
            trace = trace + jnp.where(source_ref[b : b + 1, :] - s == slot, tail[:, s : s + 1], 0.0)
        trace_ref[b : b + 1, :] = 0.5 * jnp.sum(trace, axis=0, keepdims=True)
    index = slot_columns(send_ref)
    bits = width.bit_length() - 1
    added = None
    for s in range(slots):
        column = jnp.broadcast_to(index[:, s : s + 1], (groups, width))
        choice = (lanes((groups, 2 * height)) == (column >> bits)[:, 0 : 2 * height]).astype(BF16)
        value = jnp.where(lanes((groups, width)) == (column & (width - 1)), tail[:, slots + s : slots + s + 1], 0.0)
        term = dot_exact(choice, value, ((0,), (0,)))
        added = term if added is None else added + term
    edge_x = edge_ref[0]
    edge_y = edge_ref[1]
    shape = (height, width)
    lane = lanes(shape)
    line = rows(shape)
    own = side_ref[core, chips : chips + 1, :]
    other = side_ref[core, chips + SIDE // 2 : chips + SIDE // 2 + 1, :]
    above = jnp.where(core == 0, other, own)
    below = jnp.where(core == 0, own, other)
    next_x = jnp.where(lane == width - 1, 0.0, pltpu.roll(edge_x, width - 1, 1))
    next_y = jnp.where(line == height - 1, below, pltpu.roll(edge_y, height - 1, 0))
    flux = next_y - edge_y - next_x + edge_x
    flux_left = jnp.where(lane == 0, -edge_x, pltpu.roll(flux, 1, 1))
    flux_up = jnp.where(line == 0, edge_y + above, pltpu.roll(flux, 1, 0))
    volume_ref[0] = flux_left - flux + conductance_ref[0] * edge_x + added[0:height, :]
    volume_ref[1] = flux_up - flux + conductance_ref[1] * edge_y + added[height : 2 * height, :]
    for copy in copies[-2:]:
        copy.wait()


def finish_kernel(
    members,
    chips,
    volume_in,
    trace_ref,
    index_ref,
    keep_ref,
    near_pick_ref,
    every_ref,
    near_ref,
    coupling_ref,
    left_ref,
    volume_ref,
    surface_ref,
    picked_ref,
    vector_ref,
):
    blocks, width = trace_ref.shape
    height = volume_ref.shape[1]
    rank = left_ref.shape[1]
    per_member = chips + blocks + 1
    per_core = members * per_member
    core = lax.rem(lax.axis_index("group"), CORES)
    member = lax.axis_index("member")
    near_count = near_ref.shape[1]
    far_count = coupling_ref.shape[1]
    here = side_of(member, members)
    fields = []
    for m in range(members):
        held = lax.rem(core + side_of(m, members) + here + 1, CORES)
        row = held * per_core + spot(m, FIRST_MEMBER, members) * per_member + chips
        fields.append(every_ref[pl.ds(row, blocks), :])
    choice = near_pick_ref[:, 0 : members * blocks].astype(BF16)
    vector_ref[...] = dot_exact(choice, jnp.concatenate(fields, axis=0), ((1,), (0,)))
    sums = []
    for b in range(blocks):
        total = jnp.zeros((width, width), F32)
        for n in range(near_count):
            at = b * near_count + n
            total = total + near_ref[b, n] * vector_ref[at : at + 1, :]
        sums.append(total)
    near = dot_exact(jnp.ones((8, width), BF16), jnp.concatenate(sums, axis=0), ((1,), (1,)))
    for b in range(blocks):
        for f in range(far_count):
            at = b * far_count + f
            picked_ref[at : at + 1, :] = every_ref[pl.ds(index_ref[0, at], 1), :]
    picked = jnp.where(keep_ref[...] > 0.0, picked_ref[...], 0.0)
    folded = picked
    for q in range(1, width // rank):
        folded = folded + pltpu.roll(picked, q * rank, 1)
    picked_ref[...] = folded
    for b in range(blocks):
        total = jnp.zeros((rank, rank), F32)
        for f in range(far_count):
            at = b * far_count + f
            total = total + coupling_ref[b, f] * picked_ref[at : at + 1, 0:rank]
        summed = jnp.sum(total, axis=1, keepdims=True)
        far = jnp.sum(left_ref[b] * summed, axis=0, keepdims=True)
        surface_ref[b : b + 1, :] = near[0:1, b * width : (b + 1) * width] + far + trace_ref[b : b + 1, :]

    ends = chips + blocks

    def rim_of(other):
        inside = jnp.where((other >= 0) & (other < members), 1.0, 0.0)
        other = lax.clamp(0, other, members - 1)
        held = lax.rem(core + side_of(other, members) + here + 1, CORES)
        row = spot(other, FIRST_MEMBER, members) * per_member + ends
        mine = every_ref[pl.ds(held * per_core + row, 1), :] * inside
        theirs = every_ref[pl.ds((1 - held) * per_core + row, 1), :] * inside
        return mine, theirs

    mine, theirs = rim_of(member - 1)
    mine_after, theirs_after = rim_of(member + 1)
    shape = (height, width)
    lane = lanes(shape)
    line = rows(shape)
    corner_y = 2 * height + jnp.where(core == 0, 0, 3 * height // 2)
    left = upright(mine, 0, shape)
    left = left + jnp.where(line[:, 0:1] == height - 1, upright(theirs, corner_y - height + 1, shape), 0.0)
    right = upright(mine_after, height, shape)
    corner_x = jnp.where(core == 0, 3 * height, 2 * height - 1)
    corner = jnp.sum(jnp.where(lanes((1, width)) == corner_x, theirs_after, 0.0), axis=1, keepdims=True)
    end = jnp.where(lane == width - 1, right, 0.0)
    volume_ref[0] = volume_in[0] + jnp.where(lane == 0, left, 0.0) + end
    last = jnp.where(lane == width - 1, 1.0, 0.0)
    up = jnp.where(line == 0, corner, pltpu.roll(jnp.broadcast_to(right, shape), 1, 0))
    volume_ref[1] = volume_in[1] + end - last * up


def vmem(count):
    return [pl.BlockSpec(memory_space=pltpu.VMEM)] * count


PARAMS = pltpu.CompilerParams(vmem_limit_bytes=16 * 1024 * 1024)


def body(
    edge_field,
    conductance,
    send_index,
    panel_source,
    surface_field,
    near_columns,
    near_tiles,
    far_columns,
    far_ranks,
    far_coupling,
    basis_left,
    basis_right,
):
    groups = lax.axis_size("group")
    members = lax.axis_size("member")
    slots = send_index.shape[2]
    blocks, width = surface_field.shape
    chips = groups // CORES
    per_member = chips + blocks + 1
    send = jnp.transpose(send_index, (2, 0, 1))
    right = jnp.swapaxes(basis_right, 1, 2)
    left = jnp.swapaxes(basis_left, 1, 2)
    near_count = near_columns.shape[1]
    far_count = far_columns.shape[1]
    chip_order = [(FIRST_CHIP + chip) % chips for chip in range(chips)]
    member_order = [(FIRST_MEMBER + member) % members for member in range(members)]
    one_core = [[chip * CORES + core for chip in chip_order] for core in range(CORES)]
    crossed = [
        [(chip * CORES + (core + side_of(m, members)) % CORES) * members + m for m in member_order]
        for chip in range(chips)
        for core in range(CORES)
    ]
    one_chip = [[chip * CORES + core for core in reversed(range(CORES))] for chip in range(chips)]

    hbm = pl.BlockSpec(memory_space=pltpu.HBM)
    edge_field, conductance, send, panel_source, surface_field, right, left, far_coupling = [
        pltpu.with_memory_space_constraint(array, pltpu.HBM)
        for array in (edge_field, conductance, send, panel_source, surface_field, right, left, far_coupling)
    ]
    near_columns, far_columns, far_ranks = [
        pltpu.with_memory_space_constraint(array, pltpu.HBM) for array in (near_columns, far_columns, far_ranks)
    ]

    def like(array):
        return pltpu.VMEM(array.shape, array.dtype)

    def out(*shape, dtype=F32):
        return jax.ShapeDtypeStruct(shape, dtype)

    first, rim = pl.pallas_call(
        pack_kernel,
        name="pack",
        out_shape=(out(chips * ROWS, width), out(blocks + 2, width)),
        in_specs=[hbm] * 5,
        out_specs=tuple(vmem(2)),
        scratch_shapes=[
            like(edge_field),
            like(send),
            like(panel_source),
            like(surface_field),
            like(right),
            pltpu.VMEM((groups, width), F32),
            pltpu.SemaphoreType.DMA((5,)),
        ],
        compiler_params=PARAMS,
    )(edge_field, send, panel_source, surface_field, right)
    first = lax.all_to_all(
        first.reshape(chips, 1, ROWS * width),
        "group",
        split_axis=0,
        concat_axis=0,
        axis_index_groups=one_core,
        tiled=True,
    ).reshape(chips * ROWS, width)
    second, side = pl.pallas_call(
        functools.partial(spread_kernel, members, slots),
        name="spread",
        out_shape=(out(members * per_member, width), out(chips + SIDE, width)),
        in_specs=vmem(2),
        out_specs=tuple(vmem(2)),
        scratch_shapes=[pltpu.VMEM((per_member, width), F32)],
        compiler_params=PARAMS,
    )(first, rim)
    second = lax.all_to_all(
        second.reshape(members, 1, per_member * width),
        ("group", "member"),
        split_axis=0,
        concat_axis=0,
        axis_index_groups=crossed,
        tiled=True,
    )
    side = lax.all_gather(side, "group", axis=0, axis_index_groups=one_chip, tiled=True)
    volume, trace, index, keep, near_pick, coupling, left = pl.pallas_call(
        functools.partial(local_kernel, members),
        name="local",
        out_shape=(
            out(*edge_field.shape),
            out(blocks, width),
            out(1, width, dtype=jnp.int32),
            out(blocks * far_count, width),
            out(blocks * near_count, width),
            out(*far_coupling.shape),
            out(*left.shape),
        ),
        in_specs=[hbm] * 9 + vmem(1),
        out_specs=tuple(vmem(7)),
        scratch_shapes=[
            like(edge_field),
            like(conductance),
            like(send),
            like(panel_source),
            like(near_columns),
            like(far_columns),
            like(far_ranks),
            pltpu.VMEM((groups, width), F32),
            pltpu.SemaphoreType.DMA((9,)),
        ],
        compiler_params=PARAMS,
        cost_estimate=pl.CostEstimate(flops=10_000_000, bytes_accessed=2_500_000, transcendentals=0),
    )(
        edge_field,
        conductance,
        send,
        panel_source,
        near_columns,
        far_columns,
        far_ranks,
        far_coupling,
        left,
        side.reshape(CORES, chips + SIDE, width),
    )
    every = lax.all_gather(
        second.reshape(members * per_member, width),
        "group",
        axis=0,
        axis_index_groups=one_chip,
        tiled=True,
    )
    return pl.pallas_call(
        functools.partial(finish_kernel, members, chips),
        name="finish",
        out_shape=(out(*edge_field.shape), out(blocks, width)),
        in_specs=vmem(9),
        out_specs=tuple(vmem(2)),
        scratch_shapes=[
            pltpu.VMEM((blocks * far_count, width), F32),
            pltpu.VMEM((blocks * near_count, width), F32),
        ],
        compiler_params=PARAMS,
    )(volume, trace, index, keep, near_pick, every, near_tiles, coupling, left)


def solution(mesh):
    both = ("group", "member")
    placed = (
        P(None, "group", "member"),
        P(None, "group", "member"),
        P(both, None, None),
        P(both, None),
        P(both, None),
        P(both, None),
        P(both, None, None, None),
        P(both, None),
        P(both, None),
        P(both, None, None, None),
        P(both, None, None),
        P(both, None, None),
    )
    return jax.shard_map(
        body,
        mesh=mesh,
        in_specs=placed,
        out_specs=(P(None, "group", "member"), P(both, None)),
        check_vma=False,
    )
```

```python
import functools

import jax
import jax.numpy as jnp
from jax import lax
from jax.experimental import pallas as pl
from jax.experimental.pallas import tpu as pltpu
from jax.sharding import PartitionSpec as P

F32 = jnp.float32
BF16 = jnp.bfloat16
HIGHEST = lax.Precision.HIGHEST
FIRST_CHIP = 34
FIRST_MEMBER = 4
CORES = 2
ROWS = 3
SIDE = 8


def split3(value):
    first = value.astype(BF16)
    rest = value - first.astype(F32)
    second = rest.astype(BF16)
    third = (rest - second.astype(F32)).astype(BF16)
    return first, second, third


def dot_exact(choice, value, dims):
    total = None
    for part in split3(value):
        term = lax.dot_general(choice, part, (dims, ((), ())), preferred_element_type=F32)
        total = term if total is None else total + term
    return total


def dot_full(left, right, dims):
    return lax.dot_general(left, right, (dims, ((), ())), precision=HIGHEST, preferred_element_type=F32)


def lanes(shape):
    return lax.broadcasted_iota(jnp.int32, shape, len(shape) - 1)


def rows(shape):
    return lax.broadcasted_iota(jnp.int32, shape, len(shape) - 2)


def upright(row, start, shape):
    wide = jnp.where(lanes(shape) == rows(shape) + start, row, 0.0)
    return jnp.sum(wide, axis=1, keepdims=True)


def spot(index, first, count):
    return (index + (count - first % count)) % count


def side_of(member, members):
    return 2 * member // members


def fetch(pairs, sems):
    copies = [pltpu.make_async_copy(source, target, sems.at[i]) for i, (source, target) in enumerate(pairs)]
    for copy in copies:
        copy.start()
    return copies


def slot_columns(send_ref):
    slots, _, groups = send_ref.shape
    rest = jnp.zeros((8 - slots, groups), jnp.int32)
    return jnp.concatenate([send_ref[s] for s in range(slots)] + [rest], axis=0).T


def pack_kernel(
    edge_in,
    send_in,
    source_in,
    surface_in,
    right_in,
    out_ref,
    rim_ref,
    edge_ref,
    send_ref,
    source_ref,
    surface_ref,
    right_ref,
    tail_ref,
    sems,
):
    blocks, width = surface_ref.shape
    rank = right_ref.shape[1]
    height = edge_ref.shape[1]
    slots, _, groups = send_ref.shape
    chips = groups // CORES
    bits = width.bit_length() - 1
    copies = fetch(
        (
            (edge_in, edge_ref),
            (send_in, send_ref),
            (surface_in, surface_ref),
            (source_in, source_ref),
            (right_in, right_ref),
        ),
        sems,
    )
    core = lax.rem(lax.axis_index("group"), CORES)
    for copy in copies[:2]:
        copy.wait()
    for copy in copies[2:]:
        copy.wait()
    edge_x = edge_ref[0]
    edge_y = edge_ref[1]
    last_x = edge_x[height - 1 : height, :]
    beyond = jnp.where(lanes((1, width)) == width - 1, 0.0, pltpu.roll(last_x, width - 1, 1))
    down = last_x - beyond - edge_y[height - 1 : height, :]
    rim = jnp.where(core == CORES - 1, down, edge_y[0:1, :])
    own = jnp.where(core == 0, down, edge_y[0:1, :])
    next_y = jnp.where(rows((height, width)) == height - 1, 0.0, pltpu.roll(edge_y, height - 1, 0))
    flow = next_y - edge_y + edge_x
    last = (lanes((8, width)) == width - 1).astype(BF16)
    first = (lanes((8, width)) == 0).astype(BF16)
    ends = jnp.concatenate(
        [
            dot_exact(last, flow, ((1,), (1,)))[0:1, :],
            dot_exact(first, edge_x, ((1,), (1,)))[0:1, :],
            jnp.broadcast_to(edge_y[0:1, width - 1 : width], (1, width - 2 * height)),
        ],
        axis=1,
    )
    index = slot_columns(send_ref)
    parts = split3(edge_ref[...].reshape(2 * height, width))
    lane = lanes((groups, width))
    tail = jnp.where(lane == 2 * CORES * slots, last_x[0:1, 0:1], 0.0)
    for s in range(slots):
        column = jnp.broadcast_to(index[:, s : s + 1], (groups, width))
        choice = (lanes((groups, 2 * height)) == (column >> bits)[:, 0 : 2 * height]).astype(BF16)
        picked = None
        for part in parts:
            term = lax.dot_general(choice, part, (((1,), (0,)), ((), ())), preferred_element_type=F32)
            picked = term if picked is None else picked + term
        value = jnp.sum(jnp.where(lane == (column & (width - 1)), picked, 0.0), axis=1, keepdims=True)
        tail = jnp.where(lane == s, value, tail)
    slot = rows((groups, width)) * slots
    for s in range(slots):
        total = jnp.zeros((groups, width), F32)
        for b in range(blocks):
            total = total + jnp.where(source_ref[b : b + 1, :] - s == slot, surface_ref[b : b + 1, :], 0.0)
        tail = jnp.where(lane == slots + s, jnp.sum(total, axis=1, keepdims=True), tail)
    every = dot_full(surface_ref[...], right_ref[...].reshape(blocks * rank, width), ((1,), (1,)))
    mine = lanes((blocks, blocks * rank)) // rank == rows((blocks, blocks * rank))
    coeff = jnp.sum(jnp.where(mine, every, 0.0), axis=0, keepdims=True)
    out_ref[pl.ds(0, chips, stride=ROWS), :] = jnp.broadcast_to(coeff, (chips, width))
    out_ref[pl.ds(1, chips, stride=ROWS), :] = jnp.broadcast_to(rim, (chips, width))
    tail_ref[...] = tail
    lane = lanes((chips, width))
    even = tail_ref[pl.ds(0, chips, stride=CORES), :]
    odd = tail_ref[pl.ds(1, chips, stride=CORES), :]
    moved = pltpu.roll(odd, 2 * slots, 1)
    theirs = (lane >= 2 * slots) & (lane < 2 * CORES * slots)
    both = jnp.where(theirs, moved, even)
    turn = FIRST_CHIP % chips
    out_ref[pl.ds(2, chips - turn, stride=ROWS), :] = both[turn:, :]
    out_ref[pl.ds(2 + ROWS * (chips - turn), turn, stride=ROWS), :] = both[:turn, :]
    rim_ref[0:blocks, :] = surface_ref[...]
    rim_ref[blocks : blocks + 1, :] = ends
    rim_ref[blocks + 1 : blocks + 2, :] = own


def spread_kernel(members, slots, first_ref, rim_ref, out_ref, side_ref, block_ref):
    width = rim_ref.shape[1]
    chips = first_ref.shape[0] // ROWS
    blocks = rim_ref.shape[0] - 2
    per_member = chips + blocks + 1
    group = lax.axis_index("group")
    core = lax.rem(group, CORES)
    chip = group // CORES
    before = jnp.where(chip > 0, 1.0, 0.0)
    after = jnp.where(chip + 1 < chips, 1.0, 0.0)
    chip_before = spot(lax.max(chip - 1, 0), FIRST_CHIP, chips) * ROWS
    chip_after = spot(lax.min(chip + 1, chips - 1), FIRST_CHIP, chips) * ROWS
    rim_before = first_ref[pl.ds(chip_before + 1, 1), :] * before
    rim_after = first_ref[pl.ds(chip_after + 1, 1), :] * after
    corner_before = first_ref[pl.ds(chip_before + 2, 1), :] * before
    corners = 2 * CORES * slots
    lane = lanes((1, width))
    ends = rim_ref[blocks : blocks + 1, :]
    ends = jnp.where(lane >= 3 * width // 4, corner_before[:, corners : corners + 1], ends)
    ends = jnp.where(lane >= 7 * width // 8, rim_after[:, width - 1 : width], ends)
    block_ref[0:chips, :] = first_ref[pl.ds(0, chips, stride=ROWS), :]
    block_ref[chips : chips + blocks, :] = rim_ref[0:blocks, :]
    block_ref[chips + blocks : chips + blocks + 1, :] = ends
    for m in range(members):
        out_ref[m * per_member : (m + 1) * per_member, :] = block_ref[...]
    other = jnp.where(core == 0, rim_after, rim_before)
    side_ref[0:chips, :] = first_ref[pl.ds(2, chips, stride=ROWS), :]
    half = rows((SIDE, width)) < SIDE // 2
    side_ref[chips : chips + SIDE, :] = jnp.where(half, rim_ref[blocks + 1 : blocks + 2, :], other)


def local_kernel(
    members,
    edge_in,
    conductance_in,
    send_in,
    source_in,
    near_columns_in,
    far_columns_in,
    far_ranks_in,
    coupling_in,
    left_in,
    side_ref,
    volume_ref,
    trace_ref,
    index_ref,
    keep_ref,
    near_pick_ref,
    coupling_ref,
    left_ref,
    edge_ref,
    conductance_ref,
    send_ref,
    source_ref,
    near_columns_ref,
    far_columns_ref,
    far_ranks_ref,
    tail_ref,
    sems,
):
    copies = fetch(
        (
            (edge_in, edge_ref),
            (conductance_in, conductance_ref),
            (send_in, send_ref),
            (source_in, source_ref),
            (near_columns_in, near_columns_ref),
            (far_columns_in, far_columns_ref),
            (far_ranks_in, far_ranks_ref),
            (left_in, left_ref),
            (coupling_in, coupling_ref),
        ),
        sems,
    )
    for copy in copies[:-2]:
        copy.wait()
    blocks, width = source_ref.shape
    height = edge_ref.shape[1]
    slots, _, groups = send_ref.shape
    chips = groups // CORES
    rank = left_ref.shape[1]
    core = lax.rem(lax.axis_index("group"), CORES)
    near_count = near_columns_ref.shape[1]
    far_count = far_columns_ref.shape[1]
    column = far_columns_ref[...]
    device = column // blocks
    group = device // members
    per_member = chips + blocks + 1
    owner = device % members
    here = side_of(lax.axis_index("member"), members)
    held = (group + side_of(owner, members) + here) % CORES
    owner = spot(owner, FIRST_MEMBER, members)
    place = held * (members * per_member) + owner * per_member + spot(group // CORES, FIRST_CHIP, chips)
    rest = jnp.zeros((1, width - blocks * far_count), jnp.int32)
    index_ref[...] = jnp.concatenate([place[b : b + 1, :] for b in range(blocks)] + [rest], axis=1)
    lane = lanes((far_count, width))
    for b in range(blocks):
        square = (far_count, far_count)
        side = lanes(square) == rows(square)
        packed = column[b : b + 1, :] % blocks * width + far_ranks_ref[b : b + 1, :]
        packed = jnp.sum(jnp.where(side, packed, 0).astype(F32), axis=1, keepdims=True).astype(jnp.int32)
        kept = (lane // rank == packed // width) & (lane % rank < packed % width)
        keep_ref[b * far_count : (b + 1) * far_count, :] = kept.astype(F32)
        square = (near_count, near_count)
        side = lanes(square) == rows(square)
        picked = jnp.where(side, near_columns_ref[b : b + 1, :], 0).astype(F32)
        picked = jnp.sum(picked, axis=1, keepdims=True).astype(jnp.int32)
        near_pick_ref[b * near_count : (b + 1) * near_count, :] = (lanes((near_count, width)) == picked).astype(F32)
    for c in range(CORES):
        half = side_ref[c, 0:chips, :]
        half = jnp.where(core == 0, half, pltpu.roll(half, width - 2 * slots, 1))
        turn = FIRST_CHIP % chips
        tail_ref[pl.ds(c + CORES * turn, chips - turn, stride=CORES), :] = half[: chips - turn, :]
        tail_ref[pl.ds(c, turn, stride=CORES), :] = half[chips - turn :, :]
    tail = tail_ref[...]
    slot = rows((groups, width)) * slots
    for b in range(blocks):
        trace = jnp.zeros((groups, width), F32)
        for s in range(slots):
            trace = trace + jnp.where(source_ref[b : b + 1, :] - s == slot, tail[:, s : s + 1], 0.0)
        trace_ref[b : b + 1, :] = 0.5 * jnp.sum(trace, axis=0, keepdims=True)
    index = slot_columns(send_ref)
    bits = width.bit_length() - 1
    added = None
    for s in range(slots):
        column = jnp.broadcast_to(index[:, s : s + 1], (groups, width))
        choice = (lanes((groups, 2 * height)) == (column >> bits)[:, 0 : 2 * height]).astype(BF16)
        value = jnp.where(lanes((groups, width)) == (column & (width - 1)), tail[:, slots + s : slots + s + 1], 0.0)
        term = dot_exact(choice, value, ((0,), (0,)))
        added = term if added is None else added + term
    edge_x = edge_ref[0]
    edge_y = edge_ref[1]
    shape = (height, width)
    lane = lanes(shape)
    line = rows(shape)
    own = side_ref[1 - core, chips : chips + 1, :]
    other = side_ref[1 - core, chips + SIDE // 2 : chips + SIDE // 2 + 1, :]
    above = jnp.where(core == 0, other, own)
    below = jnp.where(core == 0, own, other)
    next_x = jnp.where(lane == width - 1, 0.0, pltpu.roll(edge_x, width - 1, 1))
    next_y = jnp.where(line == height - 1, below, pltpu.roll(edge_y, height - 1, 0))
    flux = next_y - edge_y - next_x + edge_x
    flux_left = jnp.where(lane == 0, -edge_x, pltpu.roll(flux, 1, 1))
    flux_up = jnp.where(line == 0, edge_y + above, pltpu.roll(flux, 1, 0))
    volume_ref[0] = flux_left - flux + conductance_ref[0] * edge_x + added[0:height, :]
    volume_ref[1] = flux_up - flux + conductance_ref[1] * edge_y + added[height : 2 * height, :]
    for copy in copies[-2:]:
        copy.wait()


def finish_kernel(
    members,
    chips,
    volume_in,
    trace_ref,
    index_ref,
    keep_ref,
    near_pick_ref,
    every_ref,
    near_ref,
    coupling_ref,
    left_ref,
    volume_ref,
    surface_ref,
    picked_ref,
    vector_ref,
):
    blocks, width = trace_ref.shape
    height = volume_ref.shape[1]
    rank = left_ref.shape[1]
    per_member = chips + blocks + 1
    per_core = members * per_member
    core = lax.rem(lax.axis_index("group"), CORES)
    member = lax.axis_index("member")
    near_count = near_ref.shape[1]
    far_count = coupling_ref.shape[1]
    here = side_of(member, members)
    fields = []
    for m in range(members):
        held = lax.rem(core + side_of(m, members) + here, CORES)
        row = held * per_core + spot(m, FIRST_MEMBER, members) * per_member + chips
        fields.append(every_ref[pl.ds(row, blocks), :])
    choice = near_pick_ref[:, 0 : members * blocks].astype(BF16)
    vector_ref[...] = dot_exact(choice, jnp.concatenate(fields, axis=0), ((1,), (0,)))
    sums = []
    for b in range(blocks):
        total = jnp.zeros((width, width), F32)
        for n in range(near_count):
            at = b * near_count + n
            total = total + near_ref[b, n] * vector_ref[at : at + 1, :]
        sums.append(total)
    near = dot_exact(jnp.ones((8, width), BF16), jnp.concatenate(sums, axis=0), ((1,), (1,)))
    for b in range(blocks):
        for f in range(far_count):
            at = b * far_count + f
            picked_ref[at : at + 1, :] = every_ref[pl.ds(index_ref[0, at], 1), :]
    picked = jnp.where(keep_ref[...] > 0.0, picked_ref[...], 0.0)
    folded = picked
    for q in range(1, width // rank):
        folded = folded + pltpu.roll(picked, q * rank, 1)
    picked_ref[...] = folded
    for b in range(blocks):
        total = jnp.zeros((rank, rank), F32)
        for f in range(far_count):
            at = b * far_count + f
            total = total + coupling_ref[b, f] * picked_ref[at : at + 1, 0:rank]
        summed = jnp.sum(total, axis=1, keepdims=True)
        far = jnp.sum(left_ref[b] * summed, axis=0, keepdims=True)
        surface_ref[b : b + 1, :] = near[0:1, b * width : (b + 1) * width] + far + trace_ref[b : b + 1, :]

    ends = chips + blocks

    def rim_of(other):
        inside = jnp.where((other >= 0) & (other < members), 1.0, 0.0)
        other = lax.clamp(0, other, members - 1)
        held = lax.rem(core + side_of(other, members) + here, CORES)
        row = spot(other, FIRST_MEMBER, members) * per_member + ends
        mine = every_ref[pl.ds(held * per_core + row, 1), :] * inside
        theirs = every_ref[pl.ds((1 - held) * per_core + row, 1), :] * inside
        return mine, theirs

    mine, theirs = rim_of(member - 1)
    mine_after, theirs_after = rim_of(member + 1)
    shape = (height, width)
    lane = lanes(shape)
    line = rows(shape)
    corner_y = 2 * height + jnp.where(core == 0, 0, 3 * height // 2)
    left = upright(mine, 0, shape)
    left = left + jnp.where(line[:, 0:1] == height - 1, upright(theirs, corner_y - height + 1, shape), 0.0)
    right = upright(mine_after, height, shape)
    corner_x = jnp.where(core == 0, 3 * height, 2 * height - 1)
    corner = jnp.sum(jnp.where(lanes((1, width)) == corner_x, theirs_after, 0.0), axis=1, keepdims=True)
    end = jnp.where(lane == width - 1, right, 0.0)
    volume_ref[0] = volume_in[0] + jnp.where(lane == 0, left, 0.0) + end
    last = jnp.where(lane == width - 1, 1.0, 0.0)
    up = jnp.where(line == 0, corner, pltpu.roll(jnp.broadcast_to(right, shape), 1, 0))
    volume_ref[1] = volume_in[1] + end - last * up


def vmem(count):
    return [pl.BlockSpec(memory_space=pltpu.VMEM)] * count


PARAMS = pltpu.CompilerParams(vmem_limit_bytes=16 * 1024 * 1024)


def body(
    edge_field,
    conductance,
    send_index,
    panel_source,
    surface_field,
    near_columns,
    near_tiles,
    far_columns,
    far_ranks,
    far_coupling,
    basis_left,
    basis_right,
):
    groups = lax.axis_size("group")
    members = lax.axis_size("member")
    slots = send_index.shape[2]
    blocks, width = surface_field.shape
    chips = groups // CORES
    per_member = chips + blocks + 1
    send = jnp.transpose(send_index, (2, 0, 1))
    right = jnp.swapaxes(basis_right, 1, 2)
    left = jnp.swapaxes(basis_left, 1, 2)
    near_count = near_columns.shape[1]
    far_count = far_columns.shape[1]
    chip_order = [(FIRST_CHIP + chip) % chips for chip in range(chips)]
    member_order = [(FIRST_MEMBER + member) % members for member in range(members)]
    one_core = [[chip * CORES + core for chip in chip_order] for core in range(CORES)]
    crossed = [
        [(chip * CORES + (core + side_of(m, members)) % CORES) * members + m for m in member_order]
        for chip in range(chips)
        for core in range(CORES)
    ]
    one_chip = [[chip * CORES + core for core in range(CORES)] for chip in range(chips)]

    hbm = pl.BlockSpec(memory_space=pltpu.HBM)
    edge_field, conductance, send, panel_source, surface_field, right, left, far_coupling = [
        pltpu.with_memory_space_constraint(array, pltpu.HBM)
        for array in (edge_field, conductance, send, panel_source, surface_field, right, left, far_coupling)
    ]
    near_columns, far_columns, far_ranks = [
        pltpu.with_memory_space_constraint(array, pltpu.HBM) for array in (near_columns, far_columns, far_ranks)
    ]

    def like(array):
        return pltpu.VMEM(array.shape, array.dtype)

    def out(*shape, dtype=F32):
        return jax.ShapeDtypeStruct(shape, dtype)

    first, rim = pl.pallas_call(
        pack_kernel,
        name="pack",
        out_shape=(out(chips * ROWS, width), out(blocks + 2, width)),
        in_specs=[hbm] * 5,
        out_specs=tuple(vmem(2)),
        scratch_shapes=[
            like(edge_field),
            like(send),
            like(panel_source),
            like(surface_field),
            like(right),
            pltpu.VMEM((groups, width), F32),
            pltpu.SemaphoreType.DMA((5,)),
        ],
        compiler_params=PARAMS,
    )(edge_field, send, panel_source, surface_field, right)
    first = lax.all_to_all(
        first.reshape(chips, 1, ROWS * width),
        "group",
        split_axis=0,
        concat_axis=0,
        axis_index_groups=one_core,
        tiled=True,
    ).reshape(chips * ROWS, width)
    second, side = pl.pallas_call(
        functools.partial(spread_kernel, members, slots),
        name="spread",
        out_shape=(out(members * per_member, width), out(chips + SIDE, width)),
        in_specs=vmem(2),
        out_specs=tuple(vmem(2)),
        scratch_shapes=[pltpu.VMEM((per_member, width), F32)],
        compiler_params=PARAMS,
    )(first, rim)
    second = lax.all_to_all(
        second.reshape(members, 1, per_member * width),
        ("group", "member"),
        split_axis=0,
        concat_axis=0,
        axis_index_groups=crossed,
        tiled=True,
    )
    side = lax.all_gather(side, "group", axis=0, axis_index_groups=one_chip, tiled=True)
    volume, trace, index, keep, near_pick, coupling, left = pl.pallas_call(
        functools.partial(local_kernel, members),
        name="local",
        out_shape=(
            out(*edge_field.shape),
            out(blocks, width),
            out(1, width, dtype=jnp.int32),
            out(blocks * far_count, width),
            out(blocks * near_count, width),
            out(*far_coupling.shape),
            out(*left.shape),
        ),
        in_specs=[hbm] * 9 + vmem(1),
        out_specs=tuple(vmem(7)),
        scratch_shapes=[
            like(edge_field),
            like(conductance),
            like(send),
            like(panel_source),
            like(near_columns),
            like(far_columns),
            like(far_ranks),
            pltpu.VMEM((groups, width), F32),
            pltpu.SemaphoreType.DMA((9,)),
        ],
        compiler_params=PARAMS,
        cost_estimate=pl.CostEstimate(flops=10_000_000, bytes_accessed=2_500_000, transcendentals=0),
    )(
        edge_field,
        conductance,
        send,
        panel_source,
        near_columns,
        far_columns,
        far_ranks,
        far_coupling,
        left,
        side.reshape(CORES, chips + SIDE, width),
    )
    every = lax.all_gather(
        second.reshape(members * per_member, width),
        "group",
        axis=0,
        axis_index_groups=one_chip,
        tiled=True,
    )
    return pl.pallas_call(
        functools.partial(finish_kernel, members, chips),
        name="finish",
        out_shape=(out(*edge_field.shape), out(blocks, width)),
        in_specs=vmem(9),
        out_specs=tuple(vmem(2)),
        scratch_shapes=[
            pltpu.VMEM((blocks * far_count, width), F32),
            pltpu.VMEM((blocks * near_count, width), F32),
        ],
        compiler_params=PARAMS,
    )(volume, trace, index, keep, near_pick, every, near_tiles, coupling, left)


def solution(mesh):
    both = ("group", "member")
    placed = (
        P(None, "group", "member"),
        P(None, "group", "member"),
        P(both, None, None),
        P(both, None),
        P(both, None),
        P(both, None),
        P(both, None, None, None),
        P(both, None),
        P(both, None),
        P(both, None, None, None),
        P(both, None, None),
        P(both, None, None),
    )
    return jax.shard_map(
        body,
        mesh=mesh,
        in_specs=placed,
        out_specs=(P(None, "group", "member"), P(both, None)),
        check_vma=False,
    )
```
